32 devices in a mesh: row: 4 (over x, core), col: 8 (over z, y).
Axes of the slice: x: 2, y: 2, z: 4, core: 2. Of those that a mesh axis runs over, the one named last changes fastest.
Arguments:
- layer_input: bfloat16 [4224, 1024], P('col', 'row'), may hold values from -6 to 6
- w_q: bfloat16 [1024, 1024], P('col', 'row'), may hold values from -0.1875 to 0.1875
- w_k: bfloat16 [1024, 1024], P('col', 'row'), may hold values from -0.1875 to 0.1875
- w_v: bfloat16 [1024, 1024], P('col', 'row'), may hold values from -0.1875 to 0.1875
- w_o: bfloat16 [1024, 1024], P('row', 'col'), may hold values from -0.25 to 0.25
- w_gate: bfloat16 [1024, 4096], P('col', 'row'), may hold values from -0.1875 to 0.1875
- w_up: bfloat16 [1024, 4096], P('col', 'row'), may hold values from -0.1875 to 0.1875
- w_down: bfloat16 [4096, 1024], P('row', 'col'), may hold values from -0.125 to 0.125
- norm1: float32 [1024], replicated, may hold values from 0.5 to 1.5
- norm2: float32 [1024], replicated, may hold values from 0.5 to 1.5
- q_gain: float32 [1024], P('row'), may hold values from 0.5 to 1.5
- k_gain: float32 [1024], P('row'), may hold values from 0.5 to 1.5
- bias_same: float32 [16], P('row'), may hold values from -3 to 3
- bias_diff: float32 [16], P('row'), may hold values from -3 to 3
- pre_variate: int32 [8, 512], P('col'), may hold values from 0 to 7, never falling along the last dimension, each value on 1 to 128 neighbouring positions
- pre_keep: int32 [8, 512], P('col'), may hold values 0 or 1
- dec_variate: int32 [128], P('col'), may hold values from 0 to 7
- dec_len: int32 [128], P('col'), may hold values from 1 to 1023, as said below
- dec_table: int32 [128, 8], P('col'), may hold values from 0 to 31
- dec_holder: int32 [128, 1], P('col'), may hold values from 0 to 7; in each aligned block of 16 rows (0 to 15, 16 to 31, ...) at most 2 rows name the same one
- kv_pool: bfloat16 [256, 2, 128, 1024], P('col', None, None, 'row'), may hold values from -4 to 4
- page_variates: int32 [256, 128], P('col'), may hold values from 0 to 7
Outputs:
- hidden: bfloat16 [4224, 1024], P('col', 'row')
- prefill_pages: bfloat16 [32, 2, 128, 1024], P('col', None, None, 'row')
- tail_pages: bfloat16 [128, 2, 128, 1024], P('col', None, None, 'row')
The draws below stay inside these ranges and needn't reach their ends.
Inputs may be any that keep to these rules, and one draw needn't show every extreme that they name: `pre_variate`: each variate's tokens form one run of at most 128 positions. `dec_len`: some request has exactly 1023 cached tokens. `dec_table`: entries past a request's last page are unused; requests may share pages. `dec_holder`: among the 16 requests of one column group at most 2 name the same holder, a bound that some block reaches of them.
All inputs are finite; a program needn't handle non-finite values. No bound on the sum of `pre_keep` on one device may be relied on, other than what follows from the above.
Results may differ from the reference program's by a relative error of at most 0.015.
Values may be sent and summed in bfloat16 or wider, within the bound.
A program may use at most 128 MiB of HBM per device.

```python
import math
import jax
import jax.numpy as jnp
import numpy as np
from jax import lax

D = 1024
H = 16
HD = 64
FF = 4096
PRE = 512
DEC = 16
PG = 128
MAXP = 8
POOL_DEV = 32
VARS = 8
TOKENS = 4224
DEC_ALL = 128
CAP = 2
POOL = 256
MAXLEN = 1024
N_ROW = 4
N_COL = 8


def draw_dec_len(key, part):
    first_key, second_key = jax.random.split(key)
    lengths = jax.random.randint(first_key, (DEC_ALL,), 1, MAXLEN)
    longest = jax.random.randint(second_key, (), 0, DEC_ALL)
    return jnp.where(jnp.arange(DEC_ALL) == longest, MAXLEN - 1, lengths).astype(jnp.int32)


def set_ends(result, rng, low, largest):
    place = [jax.random.randint(jax.random.fold_in(rng, axis), (), 0, length) for axis, length in enumerate(result.shape)]
    main_axis = result.shape.index(max(result.shape))
    next_to = place[:main_axis] + [(place[main_axis] + 1) % result.shape[main_axis]] + place[main_axis + 1:]
    return result.at[tuple(place)].set(low).at[tuple(next_to)].set(largest)


def spiked(entries, key, source, target, parts, factor):
    def block_of(axis_at):
        return (jnp.arange(entries.shape[axis_at]) // (entries.shape[axis_at] // parts)).reshape((-1,) + (1,) * (entries.ndim - 1 - axis_at))

    first = jax.random.permutation(key, parts)[block_of(target)]
    far = (block_of(target) + parts // 2) % parts
    return jnp.where((block_of(source) == first) | (block_of(source) == far), factor * entries, entries)


def shard_levels(key, shape, cuts, least, top_value):
    def one(dim, parts):
        steps = jax.random.uniform(jax.random.fold_in(jax.random.fold_in(key, 6), dim), (parts,), jnp.float32, least / len(cuts), top_value / len(cuts))
        return jnp.repeat(jnp.exp(steps), shape[dim] // parts).reshape((-1,) + (1,) * (len(shape) - dim - 1))

    level = one(*cuts[0])
    for cut in cuts[1:]:
        level = level * one(*cut)
    return level


def length_profile(number_of, total, limit, slope):
    weights = [(1 << 20) // math.isqrt(standing ** slope) + 1 for standing in range(2, number_of + 1)]
    surplus, holding = total - limit - (number_of - 1), [1] * (number_of - 1)
    while surplus > 0:
        candidates = [i for i in range(number_of - 1) if holding[i] < limit]
        pool, remaining = sum([weights[i] for i in candidates]), surplus
        for i in candidates:
            addition = min(limit - holding[i], max(1, remaining * weights[i] // pool), surplus)
            holding[i] = holding[i] + addition
            surplus = surplus - addition
    return np.array([limit] + holding)


def uneven(stream_key, amount, total, reach, lean):
    if amount == 2:
        one = jax.random.randint(stream_key, (), max(1, total - reach), min(reach, total - 1) + 1)
        return jnp.stack([one, total - one])
    sizes = jnp.asarray(length_profile(amount, total, reach, lean), jnp.int32)
    pairs = (amount - 1) // 2
    source_of, receiver = sizes[1:1 + 2 * pairs:2], sizes[2:2 + 2 * pairs:2]
    slack = jnp.minimum(source_of - 1, reach - receiver)
    shifted = jax.random.randint(jax.random.fold_in(stream_key, 1), (pairs,), 0, 1 << 20) % (slack + 1)
    sizes = sizes.at[1:1 + 2 * pairs:2].set(source_of - shifted).at[2:2 + 2 * pairs:2].set(receiver + shifted)
    return sizes[jax.random.permutation(jax.random.fold_in(stream_key, 2), amount)]


def routed_block(stream_key, own, number, rows, number_of, top, bound, skew):
    sequence = jax.random.permutation(stream_key, number_of)
    packed, usual = portions_of(number_of, rows * top, bound, skew, True), portions_of(number_of, rows * top, bound, skew, False)
    places = jnp.arange(number_of)

    def named(tallies, offset_by):
        used = int((tallies > 0).sum())
        fixed = max(1, used // 4)
        moved = fixed + (places - fixed + offset_by * (used - fixed)) % max(1, number_of - fixed)
        return jnp.zeros((number_of,), jnp.int32).at[sequence[jnp.where(places < fixed, places, moved)]].set(jnp.asarray(tallies, jnp.int32))

    tallies = jnp.where(number % 4 == 0, named(packed, number // 4), named(usual, number - number // 4 - 1))
    mixed = jax.random.permutation(jax.random.fold_in(own, 3), number_of)
    source_of, receiver = mixed[0:number_of // 2 * 2:2], mixed[1:number_of // 2 * 2:2]
    slack = jnp.minimum(tallies[source_of] - 1, bound - tallies[receiver]) // 2
    slack = jnp.where((source_of == sequence[0]) | (receiver == sequence[0]) | (tallies[receiver] == 0), 0, jnp.maximum(slack, 0))
    moved = jax.random.randint(jax.random.fold_in(own, 4), (number_of // 2,), 0, 1 << 20) % (slack + 1)
    tallies = tallies.at[source_of].add(-moved).at[receiver].add(moved)
    items = jnp.searchsorted(jnp.cumsum(tallies), jnp.arange(rows * top), side="right").astype(jnp.int32)
    listing = items.reshape(top, rows).T
    listing = listing[jax.random.permutation(jax.random.fold_in(own, 1), rows)]
    offset_by = jax.random.randint(jax.random.fold_in(own, 2), (rows, 1), 0, top)
    return jnp.take_along_axis(listing, (jnp.arange(top)[None, :] + offset_by) % top, axis=1)


def portions_of(amount, total, limit, slope, full):
    weights = [(1 << 20) // math.isqrt(standing ** slope) + 1 for standing in range(1, amount + 1)]
    largest = limit if full else min(limit, max(-(-total // amount), total * weights[0] // sum(weights)))
    least = 1 if total - largest >= amount - 1 else 0
    holding, spare = [largest] + [least] * (amount - 1), total - largest - least * (amount - 1)
    while spare > 0:
        candidates = [i for i in range(1, amount) if holding[i] < largest] or [i for i in range(1, amount) if holding[i] < limit]
        whole, left = sum([weights[i] for i in candidates]), spare
        for i in candidates:
            more = min(limit - holding[i], max(1, left * weights[i] // whole), spare)
            holding[i] = holding[i] + more
            spare = spare - more
    return np.array(holding)


def gaussian(own_key, extent, width, most, shards=(), held_as=jnp.bfloat16):
    result = width * jax.random.normal(own_key, extent, jnp.float32)
    if shards:
        result = result * shard_levels(own_key, extent, shards, -0.22, 0.18)
    return jnp.clip(result, -most, most).astype(held_as)


def heavy_noise(own_key, dims, deviation, bound, pieces, heavy, kind=jnp.bfloat16):
    result = deviation * jax.random.normal(own_key, dims, jnp.float32)
    if pieces:
        result = result * shard_levels(own_key, dims, pieces, -0.22, 0.18)
    return jnp.clip(spiked(result, jax.random.fold_in(own_key, 3), *heavy), -bound, bound).astype(kind)


def setup_inputs(seed: int = 0) -> dict:
    key_list = jax.random.split(jax.random.key(seed), 23)
    layer_input = gaussian(key_list[0], (TOKENS, D), 1.0, 6.0, ((0, 8), (1, 4)))
    w_q = gaussian(key_list[1], (D, D), D ** -0.5, 0.1875, ((0, 8), (1, 4)))
    w_k = gaussian(key_list[2], (D, D), D ** -0.5, 0.1875, ((0, 8), (1, 4)))
    w_v = gaussian(key_list[3], (D, D), D ** -0.5, 0.1875, ((0, 8), (1, 4)))
    w_o = heavy_noise(key_list[4], (D, D), D ** -0.5, 0.25, ((0, 4), (1, 8)), (0, 1, 8, 2.0))
    w_gate = gaussian(key_list[5], (D, FF), D ** -0.5, 0.1875, ((0, 8), (1, 4)))
    w_up = gaussian(key_list[6], (D, FF), D ** -0.5, 0.1875, ((0, 8), (1, 4)))
    w_down = heavy_noise(key_list[7], (FF, D), FF ** -0.5, 0.125, ((0, 4), (1, 8)), (0, 1, 8, 2.0))
    norm1 = jnp.clip(1.0 + 0.1 * jax.random.normal(key_list[8], (D,), jnp.float32), 0.5, 1.5)
    norm2 = jnp.clip(1.0 + 0.1 * jax.random.normal(key_list[9], (D,), jnp.float32), 0.5, 1.5)
    q_gain = jnp.clip(1.0 + 0.1 * jax.random.normal(key_list[10], (D,), jnp.float32), 0.5, 1.5)
    k_gain = jnp.clip(1.0 + 0.1 * jax.random.normal(key_list[11], (D,), jnp.float32), 0.5, 1.5)
    bias_same = gaussian(key_list[12], (H,), 1.0, 3.0, ((0, 4),), jnp.float32)
    bias_diff = gaussian(key_list[13], (H,), 1.0, 3.0, ((0, 4),), jnp.float32)
    pre_variate = jax.vmap(lambda own: jnp.searchsorted(jnp.cumsum(uneven(own, VARS, PRE, 2 * PRE // VARS, 1)), jnp.arange(PRE), side="right"))(jax.random.split(key_list[14], N_COL)).reshape((N_COL, PRE)).astype(jnp.int32)
    pre_keep = set_ends((jax.random.randint(key_list[15], (N_COL, PRE), 0, 8) < 7).astype(jnp.int32), jax.random.fold_in(key_list[15], 1), 0, 1)
    dec_variate = set_ends(jax.random.randint(key_list[16], (DEC_ALL,), 0, VARS), jax.random.fold_in(key_list[16], 1), 0, VARS - 1).astype(jnp.int32)
    dec_len = draw_dec_len(jax.random.fold_in(key_list[22], 71), 0)
    dec_table = set_ends(jax.random.randint(key_list[18], (DEC_ALL, MAXP), 0, POOL_DEV), jax.random.fold_in(key_list[18], 1), 0, POOL_DEV - 1).astype(jnp.int32)
    dec_holder_keys = jax.random.split(jax.random.fold_in(key_list[19], 1), DEC_ALL // DEC)
    dec_holder_turns = jax.random.permutation(jax.random.fold_in(key_list[19], 3), DEC_ALL // DEC)
    dec_holder = jax.vmap(lambda own, number: routed_block(jax.random.fold_in(key_list[19], 2), own, number, DEC, N_COL, 1, CAP, 2))(dec_holder_keys, dec_holder_turns).reshape((DEC_ALL, 1))
    kv_pool = gaussian(key_list[20], (POOL, 2, PG, D), 1.0, 4.0, ((0, 8), (3, 4)))
    page_variates = set_ends(jax.random.randint(key_list[21], (POOL, PG), 0, VARS), jax.random.fold_in(key_list[21], 1), 0, VARS - 1).astype(jnp.int32)
    return {"layer_input": layer_input, "w_q": w_q, "w_k": w_k, "w_v": w_v, "w_o": w_o, "w_gate": w_gate, "w_up": w_up, "w_down": w_down, "norm1": norm1, "norm2": norm2, "q_gain": q_gain, "k_gain": k_gain, "bias_same": bias_same, "bias_diff": bias_diff, "pre_variate": pre_variate, "pre_keep": pre_keep, "dec_variate": dec_variate, "dec_len": dec_len, "dec_table": dec_table, "dec_holder": dec_holder, "kv_pool": kv_pool, "page_variates": page_variates}


eps = 1e-05

def norm_rows(values, gain_row):
    return values * lax.rsqrt(lax.optimization_barrier(jnp.mean(values * values, axis=-1, keepdims=True)) + eps) * gain_row

def rotate(tensor, places):
    half_size = tensor.shape[-1] // 2
    spacing = jnp.arange(half_size).astype(jnp.float32) * (2.0 / tensor.shape[-1])
    angles = places.astype(jnp.float32)[:, None] * jnp.power(10000.0, -spacing)[None, :]
    cosine = jnp.cos(angles)[:, None, :]
    sine_part = jnp.sin(angles)[:, None, :]
    lower_half = tensor[..., :half_size]
    upper_half = tensor[..., half_size:]
    return jnp.concatenate([lower_half * cosine - upper_half * sine_part, upper_half * cosine + lower_half * sine_part], axis=-1)

def segment_time(variates):
    places = jnp.arange(variates.shape[0]).astype(jnp.int32)
    run_start = jnp.concatenate([jnp.ones((1,), dtype=jnp.bool_), variates[1:] != variates[:-1]])
    starts = lax.cummax(jnp.where(run_start, places, 0).astype(jnp.int32), axis=0)
    return places - starts

def row_sum(left_rows, weight, groups):
    width_each = left_rows.shape[1] // groups
    summed = jnp.zeros((left_rows.shape[0], weight.shape[1]), jnp.float32)
    for group_index in range(groups):
        lo_col = group_index * width_each
        partial_value = jnp.dot(left_rows[:, lo_col:lo_col + width_each], weight[lo_col:lo_col + width_each], preferred_element_type=jnp.float32)
        rounded = lax.optimization_barrier(partial_value.astype(jnp.bfloat16))
        summed = summed + rounded.astype(jnp.float32)
    return summed

def reference(layer_input, w_q, w_k, w_v, w_o, w_gate, w_up, w_down, norm1, norm2, q_gain, k_gain, bias_same, bias_diff, pre_variate, pre_keep, dec_variate, dec_len, dec_table, dec_holder, kv_pool, page_variates):
    score_scale = HD ** (-0.5)
    resid_in = layer_input.astype(jnp.float32)
    normed = norm_rows(resid_in, norm1).astype(jnp.bfloat16)
    query_proj = jnp.dot(normed, w_q, preferred_element_type=jnp.float32)
    key_proj = jnp.dot(normed, w_k, preferred_element_type=jnp.float32)
    value_proj = jnp.dot(normed, w_v, preferred_element_type=jnp.float32)
    pre_times = jax.vmap(segment_time)(pre_variate)
    places = jnp.concatenate([pre_times, dec_len.reshape(N_COL, DEC)], axis=1).reshape(-1)
    query_rot = rotate(norm_rows(query_proj.reshape(-1, H, HD), q_gain.reshape(H, HD)), places).astype(jnp.bfloat16)
    key_rot = rotate(norm_rows(key_proj.reshape(-1, H, HD), k_gain.reshape(H, HD)), places).astype(jnp.bfloat16)
    value_bf = value_proj.astype(jnp.bfloat16).reshape(-1, H, HD)
    grouped_q = query_rot.reshape(N_COL, PRE + DEC, H, HD)
    grouped_k = key_rot.reshape(N_COL, PRE + DEC, H, HD)
    grouped_v = value_bf.reshape(N_COL, PRE + DEC, H, HD)

    def prefill_group(inputs):
        pre_queries, pre_keys, pre_values, variates, keep_mask = inputs
        scores = jnp.einsum('qhd,khd->hqk', pre_queries.astype(jnp.float32), pre_keys.astype(jnp.float32)) * score_scale
        same_var = variates[:, None] == variates[None, :]
        scores = scores + jnp.where(same_var[None], bias_same[:, None, None], bias_diff[:, None, None])
        allowed = (keep_mask[None, :] == 1) | (jnp.arange(PRE)[:, None] == jnp.arange(PRE)[None, :])
        exp_scores = jnp.where(allowed[None], jnp.exp(scores), 0.0)
        weights_bf = (exp_scores / lax.optimization_barrier(jnp.sum(exp_scores, axis=2, keepdims=True))).astype(jnp.bfloat16)
        return jnp.einsum('hqk,khd->qhd', weights_bf.astype(jnp.float32), pre_values.astype(jnp.float32)).astype(jnp.bfloat16)
    pre_out = lax.map(prefill_group, (grouped_q[:, :PRE], grouped_k[:, :PRE], grouped_v[:, :PRE], pre_variate, pre_keep))

    def decode_one(inputs):
        new_query, new_key, new_value, page_rows, length, variate, holder = inputs
        pool_rows = holder * POOL_DEV + page_rows
        gathered = kv_pool[pool_rows]
        cached_keys = gathered[:, 0].reshape(MAXP * PG, H, HD)
        cached_vals = gathered[:, 1].reshape(MAXP * PG, H, HD)
        key_variates = page_variates[pool_rows].reshape(MAXP * PG)
        scores = jnp.einsum('hd,khd->hk', new_query.astype(jnp.float32), cached_keys.astype(jnp.float32)) * score_scale
        scores = scores + jnp.where((key_variates == variate)[None, :], bias_same[:, None], bias_diff[:, None])
        own_score = lax.optimization_barrier(jnp.sum(new_query.astype(jnp.float32) * new_key.astype(jnp.float32), axis=1)) * score_scale + bias_same
        exp_scores = jnp.where((jnp.arange(MAXP * PG) < length)[None, :], jnp.exp(scores), 0.0)
        own_exp = jnp.exp(own_score)
        total_weight = lax.optimization_barrier(jnp.sum(exp_scores, axis=1)) + own_exp
        weights_bf = (exp_scores / total_weight[:, None]).astype(jnp.bfloat16)
        own_weight = (own_exp / total_weight).astype(jnp.bfloat16)
        attended = jnp.einsum('hk,khd->hd', weights_bf.astype(jnp.float32), cached_vals.astype(jnp.float32)) + own_weight.astype(jnp.float32)[:, None] * new_value.astype(jnp.float32)
        tail_slot = pool_rows[length // PG]
        old_page = kv_pool[tail_slot]
        hit_row = (jnp.arange(PG) == length % PG)[None, :, None]
        new_rows = jnp.stack([new_key.reshape(D), new_value.reshape(D)])[:, None, :]
        return (attended.astype(jnp.bfloat16), jnp.where(hit_row, new_rows, old_page))
    dec_queries = grouped_q[:, PRE:].reshape(N_COL * DEC, H, HD)
    dec_keys = grouped_k[:, PRE:].reshape(N_COL * DEC, H, HD)
    dec_values = grouped_v[:, PRE:].reshape(N_COL * DEC, H, HD)
    dec_out, tail_pages = lax.map(decode_one, (dec_queries, dec_keys, dec_values, dec_table, dec_len, dec_variate, dec_holder[:, 0]))
    all_attended = jnp.concatenate([pre_out.reshape(N_COL, PRE, D), dec_out.reshape(N_COL, DEC, D)], axis=1).reshape(-1, D)
    attn_total = row_sum(all_attended, w_o, N_ROW)
    resid_full = resid_in + attn_total
    ffn_input = norm_rows(resid_full, norm2).astype(jnp.bfloat16)
    gate_proj = jnp.dot(ffn_input, w_gate, preferred_element_type=jnp.float32)
    up_proj = jnp.dot(ffn_input, w_up, preferred_element_type=jnp.float32)
    hidden_units = (jax.nn.silu(gate_proj) * up_proj).astype(jnp.bfloat16)
    ffn_total = row_sum(hidden_units, w_down, N_ROW)
    hidden = (resid_full + ffn_total).astype(jnp.bfloat16)
    prefill_pages = jnp.stack([grouped_k[:, :PRE].reshape(-1, PG, D), grouped_v[:, :PRE].reshape(-1, PG, D)], axis=1)
    return (hidden, prefill_pages, tail_pages)
```

```python
import functools

import jax
import jax.numpy as jnp
from jax import lax
from jax.experimental import pallas as pl
from jax.experimental.pallas import tpu as pltpu
from jax.sharding import PartitionSpec as P

HD = 64


eps = 1e-05


def norm_rows(values, gain_row):
    return values * lax.rsqrt(jnp.mean(values * values, axis=-1, keepdims=True) + eps) * gain_row


def rotate(tensor, places):
    half_size = tensor.shape[-1] // 2
    spacing = jnp.arange(half_size).astype(jnp.float32) * (2.0 / tensor.shape[-1])
    angles = places.astype(jnp.float32)[:, None] * jnp.power(10000.0, -spacing)[None, :]
    cosine = jnp.cos(angles)[:, None, :]
    sine_part = jnp.sin(angles)[:, None, :]
    lower_half = tensor[..., :half_size]
    upper_half = tensor[..., half_size:]
    return jnp.concatenate(
        [
            lower_half * cosine - upper_half * sine_part,
            upper_half * cosine + lower_half * sine_part,
        ],
        axis=-1,
    )


def segment_time(variates):
    places = jnp.arange(variates.shape[0])
    run_start = jnp.concatenate([jnp.ones((1,), dtype=jnp.bool_), variates[1:] != variates[:-1]])
    starts = lax.cummax(jnp.where(run_start, places, 0), axis=0)
    return places - starts


def cycle_dims(count):
    inner = 1
    while inner * inner * 4 <= count:
        inner *= 2
    return count // inner, inner


def cycle_place(member, count):
    outer, inner = cycle_dims(count)
    if inner == 1:
        return member
    z, y = member // inner, member % inner
    back = outer - 1 - z
    odd = back % 2
    along = (1 - odd) * (y - 1) + odd * (inner - 1 - y)
    return jnp.where(y == 0, z, outer + back * (inner - 1) + along)


def cycle_member(place, count):
    outer, inner = cycle_dims(count)
    if inner == 1:
        return place
    rest = jnp.maximum(place - outer, 0)
    back, along = rest // (inner - 1), rest % (inner - 1)
    odd = back % 2
    y = (1 - odd) * (1 + along) + odd * (inner - 1 - along)
    return jnp.where(place < outer, place * inner, (outer - 1 - back) * inner + y)


def gather_kernel(by_rows, n_col, n_row, *refs):
    count = len(by_rows)
    x_ref, tail_ref = refs[0], refs[1]
    shards = refs[2 : 2 + count]
    x_out, tail_out = refs[2 + count], refs[3 + count]
    wholes = refs[4 + count : 4 + 2 * count]
    own_sem, x_send, x_recv, t_send, t_recv, r_send, r_recv, l_send, l_recv = refs[4 + 2 * count :]
    me = lax.axis_index("col")
    my_row = lax.axis_index("row")
    barrier = pltpu.get_barrier_semaphore()
    for step in range(1, n_col):
        pl.semaphore_signal(
            barrier,
            inc=1,
            device_id={"col": (me + step) % n_col},
            device_id_type=pl.DeviceIdType.MESH,
        )
    for step in range(1, n_row):
        pl.semaphore_signal(
            barrier,
            inc=1,
            device_id={"row": (my_row + step) % n_row},
            device_id_type=pl.DeviceIdType.MESH,
        )
    pl.semaphore_wait(barrier, n_col + n_row - 2)

    place = cycle_place(me, n_col)
    right = cycle_member((place + 1) % n_col, n_col)
    left = cycle_member((place + n_col - 1) % n_col, n_col)
    half_way = n_col // 2

    def part(index, ref, owner, low, size):
        shard = shards[index]
        if by_rows[index]:
            depth = shard.shape[0]
            start = pl.multiple_of(owner * depth + low, 16)
            return ref.at[pl.ds(start, size)]
        width = shard.shape[1]
        if width % 128:
            return ref.at[owner, pl.ds(low, size)]
        return ref.at[pl.ds(low, size), pl.ds(pl.multiple_of(owner * width, 128), width)]

    def hop(index, step, to_right):
        shift = n_col - step if to_right else step
        owner = cycle_member((place + shift) % n_col, n_col)
        depth = shards[index].shape[0]
        low, size = 0, depth
        if step == half_way - 1:
            low, size = (0, depth // 2) if to_right else (depth // 2, depth // 2)
        there = part(index, wholes[index], owner, low, size)
        here = shards[index].at[pl.ds(low, size)] if step == 0 else there
        send, recv = (r_send, r_recv) if to_right else (l_send, l_recv)
        return pltpu.make_async_remote_copy(
            src_ref=here,
            dst_ref=there,
            send_sem=send.at[index, step],
            recv_sem=recv.at[index, step],
            device_id={"col": right if to_right else left},
            device_id_type=pl.DeviceIdType.MESH,
        )

    def x_copy(step):
        width = x_ref.shape[1]
        return pltpu.make_async_remote_copy(
            src_ref=x_ref,
            dst_ref=x_out.at[:, pl.ds(pl.multiple_of(my_row * width, 128), width)],
            send_sem=x_send.at[step],
            recv_sem=x_recv.at[step],
            device_id={"row": (my_row + step) % n_row},
            device_id_type=pl.DeviceIdType.MESH,
        )

    def t_copy(step):
        peer = (me + step) % n_col
        return pltpu.make_async_remote_copy(
            src_ref=tail_ref.at[peer],
            dst_ref=tail_out.at[me],
            send_sem=t_send.at[step],
            recv_sem=t_recv.at[step],
            device_id={"col": peer},
            device_id_type=pl.DeviceIdType.MESH,
        )

    own = [
        pltpu.make_async_copy(
            shards[i], part(i, wholes[i], me, 0, shards[i].shape[0]), own_sem.at[i]
        )
        for i in range(count)
    ]
    width = x_ref.shape[1]
    own.append(
        pltpu.make_async_copy(
            x_ref,
            x_out.at[:, pl.ds(pl.multiple_of(my_row * width, 128), width)],
            own_sem.at[count],
        )
    )
    own.append(pltpu.make_async_copy(tail_ref.at[me], tail_out.at[me], own_sem.at[count + 1]))
    for index in range(count):
        hop(index, 0, True).start()
        hop(index, 0, False).start()
    for step in range(1, n_row):
        x_copy(step).start()
    for copy in own:
        copy.start()
    for step in range(1, n_col):
        t_copy(step).start()
    for step in range(half_way):
        for index in range(count):
            for to_right in (True, False):
                hop(index, step, to_right).wait_recv()
                if step + 1 < half_way:
                    hop(index, step + 1, to_right).start()
    for step in range(half_way):
        for index in range(count):
            for to_right in (True, False):
                hop(index, step, to_right).wait_send()
    for step in range(1, n_row):
        x_copy(step).wait()
    for copy in own:
        copy.wait()
    for step in range(1, n_col):
        t_copy(step).wait()


def gather_all(layer_input, tail_send, shards, by_rows):
    n_col, n_row = lax.axis_size("col"), lax.axis_size("row")
    count = len(shards)
    half_way = n_col // 2
    shapes = [
        jax.ShapeDtypeStruct((layer_input.shape[0], layer_input.shape[1] * n_row), jnp.bfloat16),
        jax.ShapeDtypeStruct(tail_send.shape, jnp.bfloat16),
    ]
    for shard, rows in zip(shards, by_rows):
        depth, width = shard.shape
        whole = (depth * n_col, width) if rows else (depth, width * n_col)
        if not rows and width % 128:
            whole = (n_col, depth, width)
        shapes.append(jax.ShapeDtypeStruct(whole, jnp.bfloat16))
    gathered = pl.pallas_call(
        functools.partial(gather_kernel, by_rows, n_col, n_row),
        out_shape=shapes,
        in_specs=[pl.BlockSpec(memory_space=pl.ANY)] * (2 + count),
        out_specs=[pl.BlockSpec(memory_space=pl.ANY)] * (2 + count),
        scratch_shapes=[
            pltpu.SemaphoreType.DMA((count + 2,)),
            pltpu.SemaphoreType.DMA((n_row,)),
            pltpu.SemaphoreType.DMA((n_row,)),
            pltpu.SemaphoreType.DMA((n_col,)),
            pltpu.SemaphoreType.DMA((n_col,)),
            pltpu.SemaphoreType.DMA((count, half_way)),
            pltpu.SemaphoreType.DMA((count, half_way)),
            pltpu.SemaphoreType.DMA((count, half_way)),
            pltpu.SemaphoreType.DMA((count, half_way)),
        ],
        compiler_params=pltpu.CompilerParams(collective_id=0, has_side_effects=True),
        name="gather_all",
    )(layer_input, tail_send, *shards)
    return [
        jnp.swapaxes(each, 0, 1).reshape(each.shape[1], -1) if index > 1 and each.ndim == 3 else each
        for index, each in enumerate(gathered)
    ]


def on_device(
    layer_input,
    w_q,
    w_k,
    w_v,
    w_o,
    w_gate,
    w_up,
    w_down,
    norm1,
    norm2,
    q_gain,
    k_gain,
    bias_same,
    bias_diff,
    pre_variate,
    pre_keep,
    dec_variate,
    dec_len,
    dec_table,
    dec_holder,
    kv_pool,
    page_variates,
):
    row_count = layer_input.shape[0]
    local_width = layer_input.shape[1]
    pre_len = pre_variate.shape[1]
    dec_count = dec_len.shape[0]
    heads_here = local_width // HD
    score_scale = HD ** (-0.5)
    pool_pages = kv_pool.shape[0]
    page_size = kv_pool.shape[2]
    page_count = dec_table.shape[1]
    peer_count = lax.axis_size("col")
    slot_count = max(2, (dec_count + peer_count - 1) // peer_count)
    holder = dec_holder[:, 0]
    onehot = (holder[:, None] == jnp.arange(peer_count)[None, :]).astype(jnp.int32)
    slot_rank = jnp.sum((jnp.cumsum(onehot, axis=0) - onehot) * onehot, axis=1)
    target = holder * slot_count + slot_rank
    int_facts = jnp.concatenate([dec_table, dec_len[:, None], dec_variate[:, None]], axis=1)
    all_slots = peer_count * slot_count
    to_slot = target[None, :] == jnp.arange(all_slots)[:, None]
    send_int = jnp.sum(jnp.where(to_slot[:, :, None], int_facts[None], 0), axis=1)
    send_int = send_int.reshape(peer_count, slot_count, page_count + 2)
    int_part = lax.all_to_all(send_int, "col", split_axis=0, concat_axis=0, tiled=True)
    slot_ints = int_part.reshape(all_slots, page_count + 2)
    slot_table = slot_ints[:, :page_count]
    slot_len = slot_ints[:, page_count]
    slot_variate = slot_ints[:, page_count + 1]
    last_place = (slot_len // page_size)[:, None] == jnp.arange(page_count)[None, :]
    last_page = jnp.sum(jnp.where(last_place, slot_table, 0), axis=1)
    tail_send = kv_pool[last_page].reshape(peer_count, slot_count, 2, page_size, local_width)

    by_rows = (True, True, True, False, True, True, False)
    gathered_input, tail_back, full_q, full_k, full_v, full_o, full_gate, full_up, full_down = (
        gather_all(
            layer_input, tail_send, (w_q, w_k, w_v, w_o, w_gate, w_up, w_down), by_rows
        )
    )
    normed = norm_rows(gathered_input.astype(jnp.float32), norm1).astype(jnp.bfloat16)
    queries = jnp.dot(normed, full_q, preferred_element_type=jnp.float32)
    keys_proj = jnp.dot(normed, full_k, preferred_element_type=jnp.float32)
    values_proj = jnp.dot(normed, full_v, preferred_element_type=jnp.float32)
    places = jnp.concatenate([segment_time(pre_variate[0]), dec_len])
    query_rot = rotate(
        norm_rows(queries.reshape(row_count, heads_here, HD), q_gain.reshape(heads_here, HD)),
        places,
    ).astype(jnp.bfloat16)
    key_rot = rotate(
        norm_rows(keys_proj.reshape(row_count, heads_here, HD), k_gain.reshape(heads_here, HD)),
        places,
    ).astype(jnp.bfloat16)
    value_bf = values_proj.astype(jnp.bfloat16).reshape(row_count, heads_here, HD)

    payload = jnp.concatenate(
        [
            query_rot[pre_len:].reshape(dec_count, local_width),
            key_rot[pre_len:].reshape(dec_count, local_width),
            value_bf[pre_len:].reshape(dec_count, local_width),
        ],
        axis=1,
    )
    send_float = jnp.dot(
        to_slot.astype(jnp.bfloat16), payload, preferred_element_type=jnp.float32
    ).astype(jnp.bfloat16)
    floats = lax.all_to_all(
        send_float.reshape(peer_count, slot_count, 3 * local_width),
        "col",
        split_axis=0,
        concat_axis=0,
        tiled=True,
    ).reshape(all_slots, 3, heads_here, HD)

    keep_mask = pre_keep[0]
    variates = pre_variate[0]
    pre_keys = key_rot[:pre_len]
    pre_values = value_bf[:pre_len]
    scores = (
        jnp.einsum("qhd,khd->hqk", query_rot[:pre_len], pre_keys, preferred_element_type=jnp.float32)
        * score_scale
    )
    same_var = variates[:, None] == variates[None, :]
    scores = scores + jnp.where(same_var[None], bias_same[:, None, None], bias_diff[:, None, None])
    allowed = (keep_mask[None, :] == 1) | (
        jnp.arange(pre_len)[:, None] == jnp.arange(pre_len)[None, :]
    )
    exp_scores = jnp.where(allowed[None], jnp.exp(scores), 0.0)
    weights_bf = (exp_scores / jnp.sum(exp_scores, axis=2, keepdims=True)).astype(jnp.bfloat16)
    outputs = jnp.einsum(
        "hqk,khd->qhd", weights_bf, pre_values, preferred_element_type=jnp.float32
    ).astype(jnp.bfloat16)
    prefill_out = outputs.reshape(pre_len, local_width)

    new_query, new_key, new_value = floats[:, 0], floats[:, 1], floats[:, 2]
    head_eye = jnp.eye(heads_here, dtype=jnp.bfloat16)
    spread = (new_query[:, :, None, :] * head_eye[None, :, :, None]).reshape(
        all_slots * heads_here, local_width
    )
    pool_keys = kv_pool[:, 0].reshape(pool_pages * page_size, local_width)
    pool_vals = kv_pool[:, 1].reshape(pool_pages * page_size, local_width)
    dec_scores = (
        lax.dot_general(
            spread, pool_keys, (((1,), (1,)), ((), ())), preferred_element_type=jnp.float32
        )
        * score_scale
    ).reshape(all_slots, heads_here, pool_pages * page_size)
    pool_page = jnp.arange(pool_pages * page_size) // page_size
    pool_row = jnp.arange(pool_pages * page_size) % page_size
    times_used = jnp.zeros((all_slots, pool_pages * page_size), jnp.float32)
    for entry in range(page_count):
        left_over = (slot_len - entry * page_size)[:, None]
        hit = (slot_table[:, entry][:, None] == pool_page[None]) & (pool_row[None] < left_over)
        times_used = times_used + hit.astype(jnp.float32)
    same_dec = page_variates.reshape(1, -1) == slot_variate[:, None]
    dec_scores = dec_scores + jnp.where(
        same_dec[:, None], bias_same[None, :, None], bias_diff[None, :, None]
    )
    dec_exp = jnp.where(
        times_used[:, None] > 0, jnp.exp(dec_scores) * times_used[:, None], 0.0
    )
    own_score = (
        jnp.sum(new_query.astype(jnp.float32) * new_key.astype(jnp.float32), axis=2) * score_scale
        + bias_same[None]
    )
    own_exp = jnp.exp(own_score)
    total_weight = jnp.sum(dec_exp, axis=2) + own_exp
    dec_weights = (dec_exp / total_weight[:, :, None]).astype(jnp.bfloat16)
    own_weight = (own_exp / total_weight).astype(jnp.bfloat16)
    mixed = jnp.dot(
        dec_weights.reshape(all_slots * heads_here, pool_pages * page_size),
        pool_vals,
        preferred_element_type=jnp.float32,
    ).reshape(all_slots, heads_here, heads_here, HD)
    attended = jnp.sum(mixed * jnp.eye(heads_here)[None, :, :, None], axis=1) + own_weight.astype(
        jnp.float32
    )[:, :, None] * new_value.astype(jnp.float32)
    back_out = lax.all_to_all(
        attended.astype(jnp.bfloat16).reshape(peer_count, slot_count, local_width),
        "col",
        split_axis=0,
        concat_axis=0,
        tiled=True,
    )
    decode_out = jnp.dot(
        to_slot.T.astype(jnp.bfloat16),
        back_out.reshape(all_slots, local_width),
        preferred_element_type=jnp.float32,
    ).astype(jnp.bfloat16)
    old_tails = tail_back.reshape(all_slots, 2, page_size, local_width)[target]
    hit_row = (jnp.arange(page_size)[None, :] == (dec_len % page_size)[:, None])[:, None, :, None]
    new_rows = payload[:, local_width:].reshape(dec_count, 2, 1, local_width)
    tail_pages = jnp.where(hit_row, new_rows, old_tails)

    all_attended = jnp.concatenate([prefill_out, decode_out], axis=0)
    partial_out = jnp.dot(all_attended, full_o, preferred_element_type=jnp.float32)
    share_start = lax.axis_index("row") * local_width
    attn_total = lax.psum(partial_out.astype(jnp.bfloat16), "row").astype(jnp.float32)
    resid_full = gathered_input.astype(jnp.float32) + attn_total
    ffn_input = norm_rows(resid_full, norm2).astype(jnp.bfloat16)
    resid_share = lax.dynamic_slice_in_dim(resid_full, share_start, local_width, 1)
    gate_proj = jnp.dot(ffn_input, full_gate, preferred_element_type=jnp.float32)
    up_proj = jnp.dot(ffn_input, full_up, preferred_element_type=jnp.float32)
    hidden_units = (jax.nn.silu(gate_proj) * up_proj).astype(jnp.bfloat16)
    partial_ffn = jnp.dot(hidden_units, full_down, preferred_element_type=jnp.float32)
    ffn_share = lax.psum_scatter(
        partial_ffn.astype(jnp.bfloat16), "row", scatter_dimension=1, tiled=True
    ).astype(jnp.float32)
    hidden = (resid_share + ffn_share).astype(jnp.bfloat16)
    prefill_pages = jnp.stack(
        [
            key_rot[:pre_len].reshape(pre_len // page_size, page_size, local_width),
            value_bf[:pre_len].reshape(pre_len // page_size, page_size, local_width),
        ],
        axis=1,
    )
    return (hidden, prefill_pages, tail_pages)


def solution(mesh):
    placed = (
        P("col", "row"),
        P("col", "row"),
        P("col", "row"),
        P("col", "row"),
        P("row", "col"),
        P("col", "row"),
        P("col", "row"),
        P("row", "col"),
        P(),
        P(),
        P("row"),
        P("row"),
        P("row"),
        P("row"),
        P("col", None),
        P("col", None),
        P("col"),
        P("col"),
        P("col", None),
        P("col", None),
        P("col", None, None, "row"),
        P("col", None),
    )
    return jax.shard_map(
        on_device,
        mesh=mesh,
        in_specs=placed,
        out_specs=(P("col", "row"), P("col", None, None, "row"), P("col", None, None, "row")),
        check_vma=False,
    )
```

```python
import functools

import jax
import jax.numpy as jnp
from jax import lax
from jax.experimental import pallas as pl
from jax.experimental.pallas import tpu as pltpu
from jax.sharding import PartitionSpec as P

HD = 64


eps = 1e-05


def norm_rows(values, gain_row):
    return values * lax.rsqrt(jnp.mean(values * values, axis=-1, keepdims=True) + eps) * gain_row


def rotate(tensor, places):
    half_size = tensor.shape[-1] // 2
    spacing = jnp.arange(half_size).astype(jnp.float32) * (2.0 / tensor.shape[-1])
    angles = places.astype(jnp.float32)[:, None] * jnp.power(10000.0, -spacing)[None, :]
    cosine = jnp.cos(angles)[:, None, :]
    sine_part = jnp.sin(angles)[:, None, :]
    lower_half = tensor[..., :half_size]
    upper_half = tensor[..., half_size:]
    return jnp.concatenate(
        [
            lower_half * cosine - upper_half * sine_part,
            upper_half * cosine + lower_half * sine_part,
        ],
        axis=-1,
    )


def segment_time(variates):
    places = jnp.arange(variates.shape[0])
    run_start = jnp.concatenate([jnp.ones((1,), dtype=jnp.bool_), variates[1:] != variates[:-1]])
    starts = lax.cummax(jnp.where(run_start, places, 0), axis=0)
    return places - starts


def cycle_dims(count):
    inner = 1
    while inner * inner * 4 <= count:
        inner *= 2
    return count // inner, inner


def cycle_place(member, count):
    outer, inner = cycle_dims(count)
    if inner == 1:
        return member
    z, y = member // inner, member % inner
    back = outer - 1 - z
    odd = back % 2
    along = (1 - odd) * (y - 1) + odd * (inner - 1 - y)
    return jnp.where(y == 0, z, outer + back * (inner - 1) + along)


def cycle_member(place, count):
    outer, inner = cycle_dims(count)
    if inner == 1:
        return place
    rest = jnp.maximum(place - outer, 0)
    back, along = rest // (inner - 1), rest % (inner - 1)
    odd = back % 2
    y = (1 - odd) * (1 + along) + odd * (inner - 1 - along)
    return jnp.where(place < outer, place * inner, (outer - 1 - back) * inner + y)


def greet(n_col, n_row):
    me, my_row = lax.axis_index("col"), lax.axis_index("row")
    barrier = pltpu.get_barrier_semaphore()
    for step in range(1, n_col):
        pl.semaphore_signal(
            barrier,
            inc=1,
            device_id={"col": (me + step) % n_col},
            device_id_type=pl.DeviceIdType.MESH,
        )
    for step in range(1, n_row):
        pl.semaphore_signal(
            barrier,
            inc=1,
            device_id={"row": (my_row + step) % n_row},
            device_id_type=pl.DeviceIdType.MESH,
        )
    pl.semaphore_wait(barrier, n_col + n_row - 2)


def ring_hops(by_rows, n_col, shards, wholes, sems):
    me = lax.axis_index("col")
    place = cycle_place(me, n_col)
    right = cycle_member((place + 1) % n_col, n_col)
    left = cycle_member((place + n_col - 1) % n_col, n_col)
    half_way = n_col // 2
    r_send, r_recv, l_send, l_recv = sems

    def part(index, owner, low, size):
        shard, ref = shards[index], wholes[index]
        if by_rows[index]:
            depth = shard.shape[0]
            start = pl.multiple_of(owner * depth + low, 16)
            return ref.at[pl.ds(start, size)]
        width = shard.shape[1]
        if width % 128:
            return ref.at[owner, pl.ds(low, size)]
        return ref.at[pl.ds(low, size), pl.ds(pl.multiple_of(owner * width, 128), width)]

    def hop(index, step, to_right):
        shift = n_col - step if to_right else step
        owner = cycle_member((place + shift) % n_col, n_col)
        depth = shards[index].shape[0]
        low, size = 0, depth
        if step == half_way - 1:
            low, size = (0, depth // 2) if to_right else (depth // 2, depth // 2)
        there = part(index, owner, low, size)
        here = shards[index].at[pl.ds(low, size)] if step == 0 else there
        send, recv = (r_send, r_recv) if to_right else (l_send, l_recv)
        return pltpu.make_async_remote_copy(
            src_ref=here,
            dst_ref=there,
            send_sem=send.at[index, step],
            recv_sem=recv.at[index, step],
            device_id={"col": right if to_right else left},
            device_id_type=pl.DeviceIdType.MESH,
        )

    def own_copy(index, sem):
        return pltpu.make_async_copy(
            shards[index], part(index, me, 0, shards[index].shape[0]), sem
        )

    return hop, own_copy


def whole_shape(shard, rows, n_col):
    depth, width = shard.shape
    if rows:
        return (depth * n_col, width)
    if width % 128:
        return (n_col, depth, width)
    return (depth, width * n_col)


def gather_kernel(by_rows, n_col, n_row, *refs):
    count = len(by_rows)
    x_ref = refs[0]
    shards = refs[1 : 1 + count]
    x_out = refs[1 + count]
    wholes = refs[2 + count : 2 + 2 * count]
    own_sem, x_send, x_recv = refs[2 + 2 * count : 5 + 2 * count]
    my_row = lax.axis_index("row")
    half_way = n_col // 2
    greet(n_col, n_row)
    hop, own_copy = ring_hops(by_rows, n_col, shards, wholes, refs[5 + 2 * count :])
    width = x_ref.shape[1]
    x_place = x_out.at[:, pl.ds(pl.multiple_of(my_row * width, 128), width)]

    def x_copy(step):
        return pltpu.make_async_remote_copy(
            src_ref=x_ref,
            dst_ref=x_place,
            send_sem=x_send.at[step],
            recv_sem=x_recv.at[step],
            device_id={"row": (my_row + step) % n_row},
            device_id_type=pl.DeviceIdType.MESH,
        )

    own = [own_copy(i, own_sem.at[i]) for i in range(count)]
    own.append(pltpu.make_async_copy(x_ref, x_place, own_sem.at[count]))
    for index in range(count):
        hop(index, 0, True).start()
        hop(index, 0, False).start()
    for step in range(1, n_row):
        x_copy(step).start()
    for copy in own:
        copy.start()
    for step in range(half_way):
        for index in range(count):
            for to_right in (True, False):
                hop(index, step, to_right).wait_recv()
                if step + 1 < half_way:
                    hop(index, step + 1, to_right).start()
    for step in range(half_way):
        for index in range(count):
            for to_right in (True, False):
                hop(index, step, to_right).wait_send()
    for step in range(1, n_row):
        x_copy(step).wait()
    for copy in own:
        copy.wait()


def gather_all(layer_input, shards, by_rows):
    n_col, n_row = lax.axis_size("col"), lax.axis_size("row")
    count = len(shards)
    half_way = n_col // 2
    shapes = [
        jax.ShapeDtypeStruct((layer_input.shape[0], layer_input.shape[1] * n_row), jnp.bfloat16)
    ] + [
        jax.ShapeDtypeStruct(whole_shape(shard, rows, n_col), jnp.bfloat16)
        for shard, rows in zip(shards, by_rows)
    ]
    return pl.pallas_call(
        functools.partial(gather_kernel, by_rows, n_col, n_row),
        out_shape=shapes,
        in_specs=[pl.BlockSpec(memory_space=pl.ANY)] * (1 + count),
        out_specs=[pl.BlockSpec(memory_space=pl.ANY)] * (1 + count),
        scratch_shapes=[
            pltpu.SemaphoreType.DMA((count + 1,)),
            pltpu.SemaphoreType.DMA((n_row,)),
            pltpu.SemaphoreType.DMA((n_row,)),
        ]
        + [pltpu.SemaphoreType.DMA((count, half_way))] * 4,
        compiler_params=pltpu.CompilerParams(collective_id=0, has_side_effects=True),
        name="gather_all",
    )(layer_input, *shards)


NT = (((1,), (1,)), ((), ()))


def columns_of(ref, index, width):
    if len(ref.shape) == 3:
        each = width // ref.shape[2]
        return jnp.concatenate([ref[index * each + i] for i in range(each)], axis=1)
    return ref[:, index * width : (index + 1) * width]


def layer_kernel(dims, *refs):
    n_col, n_row, heads, dec_count, page_count, score_scale = dims
    (
        bias_ref,
        q_ref,
        k_ref,
        v_ref,
        var_col,
        var_row,
        keep_row,
        ask_ref,
        facts_ref,
        slot_bias,
        page_var,
        pool_ref,
        pick_ref,
        own_ref,
        x_ref,
        norm_ref,
        wo_ref,
        wg_shard,
        wu_shard,
        wd_shard,
        tail_ref,
        hidden_ref,
        tail_out,
        wg_ref,
        wu_ref,
        wd_ref,
        asked,
        answer,
        answered,
        attended,
        part_send,
        part_recv,
        resid_all,
        normed,
        units,
        resid,
        own_sem,
        ask_send,
        ask_recv,
        ans_send,
        ans_recv,
        t_send,
        t_recv,
        row_send,
        row_recv,
        r_send,
        r_recv,
        l_send,
        l_recv,
    ) = refs
    me, my_row = lax.axis_index("col"), lax.axis_index("row")
    half_way = n_col // 2
    rows, width = x_ref.shape
    pre_len = rows - dec_count
    greet(n_col, n_row)
    hop, own_copy = ring_hops(
        (True, True, False),
        n_col,
        (wg_shard, wu_shard, wd_shard),
        (wg_ref, wu_ref, wd_ref),
        (r_send, r_recv, l_send, l_recv),
    )

    def to_peer(src, dst, send, recv, step):
        return pltpu.make_async_remote_copy(
            src_ref=src,
            dst_ref=dst,
            send_sem=send.at[step],
            recv_sem=recv.at[step],
            device_id={"col": (me + step) % n_col},
            device_id_type=pl.DeviceIdType.MESH,
        )

    def ask(step):
        return to_peer(
            ask_ref.at[(me + step) % n_col], asked.at[me], ask_send, ask_recv, step
        )

    def reply(step):
        return to_peer(
            answer.at[(me + step) % n_col], answered.at[me], ans_send, ans_recv, step
        )

    def tail(step):
        return to_peer(tail_ref.at[(me + step) % n_col], tail_out.at[me], t_send, t_recv, step)

    def to_row(src, dst, stage, step):
        return pltpu.make_async_remote_copy(
            src_ref=src,
            dst_ref=dst,
            send_sem=row_send.at[stage, step],
            recv_sem=row_recv.at[stage, step],
            device_id={"row": (my_row + step) % n_row},
            device_id_type=pl.DeviceIdType.MESH,
        )

    def scatter(stage, step):
        return to_row(
            part_send.at[stage, (my_row + step) % n_row],
            part_recv.at[stage, my_row],
            stage,
            step,
        )

    def spread(step):
        return to_row(resid_all.at[my_row], resid_all.at[my_row], 2, step)

    def pump(step):
        for index in range(3):
            for to_right in (True, False):
                hop(index, step, to_right).wait_recv()
                if step + 1 < half_way:
                    hop(index, step + 1, to_right).start()

    own_ask = pltpu.make_async_copy(ask_ref.at[me], asked.at[me], own_sem.at[3])
    own_tail = pltpu.make_async_copy(tail_ref.at[me], tail_out.at[me], own_sem.at[4])
    for step in range(1, n_col):
        ask(step).start()
    own_ask.start()
    for index in range(3):
        hop(index, 0, True).start()
        hop(index, 0, False).start()
    for index in range(3):
        own_copy(index, own_sem.at[index]).start()
    own_tail.start()

    block = 128
    lane_head = lax.broadcasted_iota(jnp.int32, (block, width), 1) // HD

    @pl.loop(0, pre_len // block)
    def _(at):
        start = pl.multiple_of(at * block, block)
        queries = q_ref[pl.ds(start, block), :]
        same = var_col[pl.ds(start, block), :] == var_row[...]
        query_at = lax.broadcasted_iota(jnp.int32, (block, pre_len), 0) + start
        key_at = lax.broadcasted_iota(jnp.int32, (block, pre_len), 1)
        allowed = (keep_row[...] == 1) | (query_at == key_at)
        result = jnp.zeros((block, width), jnp.float32)
        for head in range(heads):
            one = jnp.where(lane_head == head, queries.astype(jnp.float32), 0.0)
            scores = lax.dot_general(
                one.astype(jnp.bfloat16),
                k_ref[0:pre_len, :],
                NT,
                preferred_element_type=jnp.float32,
            )
            scores = scores * score_scale + jnp.where(same, bias_ref[0, head], bias_ref[1, head])
            weights = jnp.where(allowed, jnp.exp(scores), 0.0)
            weights = weights / jnp.sum(weights, axis=1, keepdims=True)
            mixed = jnp.dot(
                weights.astype(jnp.bfloat16),
                v_ref[0:pre_len, :],
                preferred_element_type=jnp.float32,
            )
            result = jnp.where(lane_head == head, mixed, result)
        attended[pl.ds(start, block), :] = result.astype(jnp.bfloat16)

    own_ask.wait()
    for step in range(1, n_col):
        ask(step).wait_recv()
    slots, page_size = asked.shape[0] * asked.shape[1], pool_ref.shape[2]
    queries = asked[...].reshape(slots, width).astype(jnp.bfloat16)
    facts = facts_ref[...]
    length = facts[:, page_count : page_count + 1]
    variate = facts[:, page_count + 1 : page_count + 2]
    same_bias, diff_bias = slot_bias[:, 0:1], slot_bias[:, 1:2]
    row_at = lax.broadcasted_iota(jnp.int32, (slots, page_size), 1)

    def one_page(page, carry):
        acc, total = carry
        scores = lax.dot_general(
            queries, pool_ref[page, 0], NT, preferred_element_type=jnp.float32
        )
        same = page_var[pl.ds(page, 1), :] == variate
        scores = scores * score_scale + jnp.where(same, same_bias, diff_bias)
        used = jnp.zeros((slots, page_size), jnp.float32)
        for entry in range(page_count):
            left_over = jnp.where(
                facts[:, entry : entry + 1] == page, length - entry * page_size, 0
            )
            used = used + jnp.where(row_at < left_over, 1.0, 0.0)
        weights = jnp.where(used > 0.0, used * jnp.exp(scores), 0.0)
        total = total + jnp.sum(weights, axis=1, keepdims=True)
        acc = acc + jnp.dot(
            weights.astype(jnp.bfloat16), pool_ref[page, 1], preferred_element_type=jnp.float32
        )
        return acc, total

    acc, total = lax.fori_loop(
        0,
        pool_ref.shape[0],
        one_page,
        (jnp.zeros((slots, width), jnp.float32), jnp.zeros((slots, 1), jnp.float32)),
    )
    mean = jnp.where(total > 0.0, acc / jnp.where(total > 0.0, total, 1.0), 0.0)
    answer[:, :, 0:width] = mean.reshape(n_col, slots // n_col, width)
    answer[:, :, width:] = jnp.broadcast_to(total, (slots, 128)).reshape(
        n_col, slots // n_col, 128
    )
    own_reply = pltpu.make_async_copy(answer.at[me], answered.at[me], own_sem.at[5])
    own_reply.start()
    for step in range(1, n_col):
        reply(step).start()
    pump(0)
    own_reply.wait()
    for step in range(1, n_col):
        reply(step).wait_recv()
    back = answered[...].reshape(slots, width + 128)
    slot_head = (lax.broadcasted_iota(jnp.int32, (slots, width), 0) % (slots // n_col)) % heads
    mine = lax.broadcasted_iota(jnp.int32, (slots, width), 1) // HD == slot_head
    pick = pick_ref[...]
    cached = jnp.dot(
        pick,
        jnp.where(mine, back[:, 0:width], 0.0),
        preferred_element_type=jnp.float32,
        precision=lax.Precision.HIGHEST,
    )
    cached_total = jnp.dot(
        pick,
        jnp.where(mine, jnp.broadcast_to(back[:, width : width + 1], (slots, width)), 0.0),
        preferred_element_type=jnp.float32,
        precision=lax.Precision.HIGHEST,
    )
    own_exp = own_ref[...]
    whole_total = cached_total + own_exp
    attended[pl.ds(pre_len, dec_count), :] = (
        cached * (cached_total / whole_total)
        + v_ref[pre_len:rows, :].astype(jnp.float32) * (own_exp / whole_total)
    ).astype(jnp.bfloat16)

    for target in range(n_row):
        part_send[0, target] = jnp.dot(
            attended[...], columns_of(wo_ref, target, width), preferred_element_type=jnp.float32
        ).astype(jnp.bfloat16)
    for step in range(1, n_row):
        scatter(0, step).start()
    pump(1)
    total_share = part_send[0, my_row].astype(jnp.float32) + x_ref[...].astype(jnp.float32)
    for step in range(1, n_row):
        scatter(0, step).wait_recv()
    for step in range(1, n_row):
        total_share = total_share + part_recv[0, (my_row + step) % n_row].astype(jnp.float32)
    resid[...] = total_share
    resid_all[my_row] = total_share.astype(jnp.bfloat16)
    for step in range(1, n_row):
        spread(step).start()
    for step in range(2, half_way):
        pump(step)
    for step in range(1, n_col):
        tail(step).start()
    for step in range(1, n_row):
        spread(step).wait_recv()
    squares = jnp.zeros((rows, 1), jnp.float32)
    for piece in range(n_row):
        values = resid_all[piece].astype(jnp.float32)
        squares = squares + jnp.sum(values * values, axis=1, keepdims=True)
    scale = lax.rsqrt(squares * (1.0 / (n_row * width)) + eps)
    for piece in range(n_row):
        cols = slice(piece * width, (piece + 1) * width)
        normed[:, cols] = (
            resid_all[piece].astype(jnp.float32) * scale * norm_ref[:, cols]
        ).astype(jnp.bfloat16)
    for index in range(3):
        own_copy(index, own_sem.at[index]).wait()

    tile = 256

    @pl.loop(0, units.shape[1] // tile)
    def _(at):
        cols = pl.ds(pl.multiple_of(at * tile, tile), tile)
        gate = jnp.dot(normed[...], wg_ref[:, cols], preferred_element_type=jnp.float32)
        up = jnp.dot(normed[...], wu_ref[:, cols], preferred_element_type=jnp.float32)
        units[:, cols] = (gate / (1.0 + jnp.exp(-gate)) * up).astype(jnp.bfloat16)

    for target in range(n_row):
        part_send[1, target] = jnp.dot(
            units[...], columns_of(wd_ref, target, width), preferred_element_type=jnp.float32
        ).astype(jnp.bfloat16)
    for step in range(1, n_row):
        scatter(1, step).start()
    total_share = resid[...] + part_send[1, my_row].astype(jnp.float32)
    for step in range(1, n_row):
        scatter(1, step).wait_recv()
    for step in range(1, n_row):
        total_share = total_share + part_recv[1, (my_row + step) % n_row].astype(jnp.float32)
    hidden_ref[...] = total_share.astype(jnp.bfloat16)

    for step in range(1, n_row):
        scatter(0, step).wait_send()
        scatter(1, step).wait_send()
        spread(step).wait_send()
    for step in range(1, n_col):
        ask(step).wait_send()
        reply(step).wait_send()
    for step in range(half_way):
        for index in range(3):
            for to_right in (True, False):
                hop(index, step, to_right).wait_send()
    own_tail.wait()
    for step in range(1, n_col):
        tail(step).wait()


def rest_of_layer(dims, *operands):
    n_col, n_row = dims[:2]
    x, wg, wu, wd, tails = operands[14], operands[17], operands[18], operands[19], operands[20]
    ask = operands[7]
    rows, width = x.shape
    half_way = n_col // 2
    full = n_row * width
    vmem = pl.BlockSpec(memory_space=pltpu.VMEM)
    anywhere = pl.BlockSpec(memory_space=pl.ANY)
    dma = pltpu.SemaphoreType.DMA
    return pl.pallas_call(
        functools.partial(layer_kernel, dims),
        out_shape=[
            jax.ShapeDtypeStruct((rows, width), jnp.bfloat16),
            jax.ShapeDtypeStruct(tails.shape, jnp.bfloat16),
        ],
        in_specs=[pl.BlockSpec(memory_space=pltpu.SMEM)] + [vmem] * 19 + [anywhere],
        out_specs=[vmem, anywhere],
        scratch_shapes=[
            pltpu.VMEM(whole_shape(wg, True, n_col), jnp.bfloat16),
            pltpu.VMEM(whole_shape(wu, True, n_col), jnp.bfloat16),
            pltpu.VMEM(whole_shape(wd, False, n_col), jnp.bfloat16),
            pltpu.VMEM(ask.shape, jnp.float32),
            pltpu.VMEM(ask.shape[:2] + (width + 128,), jnp.float32),
            pltpu.VMEM(ask.shape[:2] + (width + 128,), jnp.float32),
            pltpu.VMEM((rows, width), jnp.bfloat16),
            pltpu.VMEM((2, n_row, rows, width), jnp.bfloat16),
            pltpu.VMEM((2, n_row, rows, width), jnp.bfloat16),
            pltpu.VMEM((n_row, rows, width), jnp.bfloat16),
            pltpu.VMEM((rows, full), jnp.bfloat16),
            pltpu.VMEM((rows, wg.shape[1]), jnp.bfloat16),
            pltpu.VMEM((rows, width), jnp.float32),
            dma((6,)),
        ]
        + [dma((n_col,))] * 6
        + [dma((3, n_row))] * 2
        + [dma((3, half_way))] * 4,
        compiler_params=pltpu.CompilerParams(
            collective_id=1, has_side_effects=True, vmem_limit_bytes=50 * 1024 * 1024
        ),
        name="rest_of_layer",
    )(*operands)


def on_device(
    layer_input,
    w_q,
    w_k,
    w_v,
    w_o,
    w_gate,
    w_up,
    w_down,
    norm1,
    norm2,
    q_gain,
    k_gain,
    bias_same,
    bias_diff,
    pre_variate,
    pre_keep,
    dec_variate,
    dec_len,
    dec_table,
    dec_holder,
    kv_pool,
    page_variates,
):
    row_count = layer_input.shape[0]
    local_width = layer_input.shape[1]
    pre_len = pre_variate.shape[1]
    dec_count = dec_len.shape[0]
    heads_here = local_width // HD
    score_scale = HD ** (-0.5)
    page_size = kv_pool.shape[2]
    page_count = dec_table.shape[1]
    peer_count = lax.axis_size("col")
    slot_count = max(2, (dec_count + peer_count - 1) // peer_count)
    holder = dec_holder[:, 0]
    onehot = (holder[:, None] == jnp.arange(peer_count)[None, :]).astype(jnp.int32)
    slot_rank = jnp.sum((jnp.cumsum(onehot, axis=0) - onehot) * onehot, axis=1)
    target = holder * slot_count + slot_rank
    int_facts = jnp.concatenate([dec_table, dec_len[:, None], dec_variate[:, None]], axis=1)
    all_slots = peer_count * slot_count
    to_slot = target[None, :] == jnp.arange(all_slots)[:, None]
    send_int = jnp.sum(jnp.where(to_slot[:, :, None], int_facts[None], 0), axis=1)
    send_int = send_int.reshape(peer_count, slot_count, page_count + 2)
    int_part = lax.all_to_all(send_int, "col", split_axis=0, concat_axis=0, tiled=True)
    slot_ints = int_part.reshape(all_slots, page_count + 2)
    slot_table = slot_ints[:, :page_count]
    slot_len = slot_ints[:, page_count]
    slot_variate = slot_ints[:, page_count + 1]
    last_place = (slot_len // page_size)[:, None] == jnp.arange(page_count)[None, :]
    last_page = jnp.sum(jnp.where(last_place, slot_table, 0), axis=1)
    tail_send = kv_pool[last_page].reshape(peer_count, slot_count, 2, page_size, local_width)

    gathered_input, full_q, full_k, full_v, full_o = gather_all(
        layer_input, (w_q, w_k, w_v, w_o), (True, True, True, False)
    )
    normed = norm_rows(gathered_input.astype(jnp.float32), norm1).astype(jnp.bfloat16)
    queries = jnp.dot(normed, full_q, preferred_element_type=jnp.float32)
    keys_proj = jnp.dot(normed, full_k, preferred_element_type=jnp.float32)
    values_proj = jnp.dot(normed, full_v, preferred_element_type=jnp.float32)
    places = jnp.concatenate([segment_time(pre_variate[0]), dec_len])
    query_rot = rotate(
        norm_rows(queries.reshape(row_count, heads_here, HD), q_gain.reshape(heads_here, HD)),
        places,
    ).astype(jnp.bfloat16)
    key_rot = rotate(
        norm_rows(keys_proj.reshape(row_count, heads_here, HD), k_gain.reshape(heads_here, HD)),
        places,
    ).astype(jnp.bfloat16)
    value_bf = values_proj.astype(jnp.bfloat16).reshape(row_count, heads_here, HD)

    flat_query = query_rot.reshape(row_count, local_width)
    flat_key = key_rot.reshape(row_count, local_width)
    flat_value = value_bf.reshape(row_count, local_width)

    used_rows = slot_count * heads_here
    slot_rows = -(-used_rows // 8) * 8
    sent_query = jnp.dot(
        to_slot.astype(jnp.bfloat16), flat_query[pre_len:], preferred_element_type=jnp.float32
    )
    lane_head = jnp.arange(local_width) // HD
    head_rows = (jnp.arange(heads_here)[:, None] == lane_head[None, :]).astype(jnp.float32)
    ask = (sent_query[:, None, :] * head_rows[None]).reshape(peer_count, used_rows, local_width)
    ask = jnp.pad(ask, ((0, 0), (0, slot_rows - used_rows), (0, 0)))

    def per_row(values):
        wide = jnp.broadcast_to(
            values.reshape(peer_count, slot_count, 1, -1),
            (peer_count, slot_count, heads_here, values.shape[-1]),
        ).reshape(peer_count, used_rows, -1)
        wide = jnp.pad(wide, ((0, 0), (0, slot_rows - used_rows), (0, 0)))
        return wide.reshape(peer_count * slot_rows, -1)

    facts = per_row(slot_ints)
    bias_pair = jnp.stack([bias_same, bias_diff], axis=1)
    slot_bias = jnp.tile(
        jnp.pad(jnp.tile(bias_pair, (slot_count, 1)), ((0, slot_rows - used_rows), (0, 0))),
        (peer_count, 1),
    )
    pick = per_row(to_slot.astype(jnp.float32)).T
    own_score = (
        jnp.sum(
            query_rot[pre_len:].astype(jnp.float32) * key_rot[pre_len:].astype(jnp.float32), axis=2
        )
        * score_scale
        + bias_same[None]
    )
    own_exp = jnp.repeat(jnp.exp(own_score), HD, axis=1)
    hidden, tail_back = rest_of_layer(
        (peer_count, lax.axis_size("row"), heads_here, dec_count, page_count, score_scale),
        jnp.stack([bias_same, bias_diff]),
        flat_query,
        flat_key,
        flat_value,
        pre_variate[0][:, None],
        pre_variate,
        pre_keep,
        ask,
        facts,
        slot_bias,
        page_variates,
        kv_pool,
        pick,
        own_exp,
        layer_input,
        norm2[None],
        full_o,
        w_gate,
        w_up,
        w_down,
        tail_send,
    )
    old_tails = tail_back.reshape(all_slots, 2, page_size, local_width)[target]
    hit_row = (jnp.arange(page_size)[None, :] == (dec_len % page_size)[:, None])[:, None, :, None]
    new_rows = jnp.stack([flat_key[pre_len:], flat_value[pre_len:]], axis=1)[:, :, None, :]
    tail_pages = jnp.where(hit_row, new_rows, old_tails)
    prefill_pages = jnp.stack(
        [
            key_rot[:pre_len].reshape(pre_len // page_size, page_size, local_width),
            value_bf[:pre_len].reshape(pre_len // page_size, page_size, local_width),
        ],
        axis=1,
    )
    return (hidden, prefill_pages, tail_pages)


def solution(mesh):
    placed = (
        P("col", "row"),
        P("col", "row"),
        P("col", "row"),
        P("col", "row"),
        P("row", "col"),
        P("col", "row"),
        P("col", "row"),
        P("row", "col"),
        P(),
        P(),
        P("row"),
        P("row"),
        P("row"),
        P("row"),
        P("col", None),
        P("col", None),
        P("col"),
        P("col"),
        P("col", None),
        P("col", None),
        P("col", None, None, "row"),
        P("col", None),
    )
    return jax.shard_map(
        on_device,
        mesh=mesh,
        in_specs=placed,
        out_specs=(P("col", "row"), P("col", None, None, "row"), P("col", None, None, "row")),
        check_vma=False,
    )
```

```python
import functools

import jax
import jax.numpy as jnp
from jax import lax
from jax.experimental import pallas as pl
from jax.experimental.pallas import tpu as pltpu
from jax.sharding import PartitionSpec as P

HD = 64


eps = 1e-05


def norm_rows(values, gain_row):
    return values * lax.rsqrt(jnp.mean(values * values, axis=-1, keepdims=True) + eps) * gain_row


def rotate(tensor, places):
    half_size = tensor.shape[-1] // 2
    spacing = jnp.arange(half_size).astype(jnp.float32) * (2.0 / tensor.shape[-1])
    angles = places.astype(jnp.float32)[:, None] * jnp.power(10000.0, -spacing)[None, :]
    cosine = jnp.cos(angles)[:, None, :]
    sine_part = jnp.sin(angles)[:, None, :]
    lower_half = tensor[..., :half_size]
    upper_half = tensor[..., half_size:]
    return jnp.concatenate(
        [
            lower_half * cosine - upper_half * sine_part,
            upper_half * cosine + lower_half * sine_part,
        ],
        axis=-1,
    )


def segment_time(variates):
    places = jnp.arange(variates.shape[0])
    run_start = jnp.concatenate([jnp.ones((1,), dtype=jnp.bool_), variates[1:] != variates[:-1]])
    starts = lax.cummax(jnp.where(run_start, places, 0), axis=0)
    return places - starts


def cycle_dims(count):
    inner = 1
    while inner * inner * 4 <= count:
        inner *= 2
    return count // inner, inner


def cycle_place(member, count):
    outer, inner = cycle_dims(count)
    if inner == 1:
        return member
    z, y = member // inner, member % inner
    back = outer - 1 - z
    odd = back % 2
    along = (1 - odd) * (y - 1) + odd * (inner - 1 - y)
    return jnp.where(y == 0, z, outer + back * (inner - 1) + along)


def cycle_member(place, count):
    outer, inner = cycle_dims(count)
    if inner == 1:
        return place
    rest = jnp.maximum(place - outer, 0)
    back, along = rest // (inner - 1), rest % (inner - 1)
    odd = back % 2
    y = (1 - odd) * (1 + along) + odd * (inner - 1 - along)
    return jnp.where(place < outer, place * inner, (outer - 1 - back) * inner + y)


def greet(n_col, n_row):
    me, my_row = lax.axis_index("col"), lax.axis_index("row")
    barrier = pltpu.get_barrier_semaphore()
    for step in range(1, n_col):
        pl.semaphore_signal(
            barrier,
            inc=1,
            device_id={"col": (me + step) % n_col},
            device_id_type=pl.DeviceIdType.MESH,
        )
    for step in range(1, n_row):
        pl.semaphore_signal(
            barrier,
            inc=1,
            device_id={"row": (my_row + step) % n_row},
            device_id_type=pl.DeviceIdType.MESH,
        )
    pl.semaphore_wait(barrier, n_col + n_row - 2)


def ring_hops(by_rows, n_col, shards, wholes, sems):
    me = lax.axis_index("col")
    place = cycle_place(me, n_col)
    right = cycle_member((place + 1) % n_col, n_col)
    left = cycle_member((place + n_col - 1) % n_col, n_col)
    half_way = n_col // 2
    r_send, r_recv, l_send, l_recv = sems

    def part(index, owner, low, size):
        shard, ref = shards[index], wholes[index]
        if by_rows[index]:
            depth = shard.shape[0]
            start = pl.multiple_of(owner * depth + low, 16)
            return ref.at[pl.ds(start, size)]
        width = shard.shape[1]
        if width % 128:
            return ref.at[owner, pl.ds(low, size)]
        return ref.at[pl.ds(low, size), pl.ds(pl.multiple_of(owner * width, 128), width)]

    def hop(index, step, to_right):
        shift = n_col - step if to_right else step
        owner = cycle_member((place + shift) % n_col, n_col)
        depth = shards[index].shape[0]
        low, size = 0, depth
        if step == half_way - 1:
            low, size = (0, depth // 2) if to_right else (depth // 2, depth // 2)
        there = part(index, owner, low, size)
        here = shards[index].at[pl.ds(low, size)] if step == 0 else there
        send, recv = (r_send, r_recv) if to_right else (l_send, l_recv)
        return pltpu.make_async_remote_copy(
            src_ref=here,
            dst_ref=there,
            send_sem=send.at[index, step],
            recv_sem=recv.at[index, step],
            device_id={"col": right if to_right else left},
            device_id_type=pl.DeviceIdType.MESH,
        )

    def own_copy(index, sem):
        return pltpu.make_async_copy(
            shards[index], part(index, me, 0, shards[index].shape[0]), sem
        )

    return hop, own_copy


def whole_shape(shard, rows, n_col):
    depth, width = shard.shape
    if rows:
        return (depth * n_col, width)
    if width % 128:
        return (n_col, depth, width)
    return (depth, width * n_col)


def gather_kernel(by_rows, n_col, n_row, *refs):
    count = len(by_rows)
    x_ref = refs[0]
    shards = refs[1 : 1 + count]
    x_out = refs[1 + count]
    wholes = refs[2 + count : 2 + 2 * count]
    own_sem, x_send, x_recv = refs[2 + 2 * count : 5 + 2 * count]
    my_row = lax.axis_index("row")
    half_way = n_col // 2
    greet(n_col, n_row)
    hop, own_copy = ring_hops(by_rows, n_col, shards, wholes, refs[5 + 2 * count :])
    width = x_ref.shape[1]
    x_place = x_out.at[:, pl.ds(pl.multiple_of(my_row * width, 128), width)]

    def x_copy(step):
        return pltpu.make_async_remote_copy(
            src_ref=x_ref,
            dst_ref=x_place,
            send_sem=x_send.at[step],
            recv_sem=x_recv.at[step],
            device_id={"row": (my_row + step) % n_row},
            device_id_type=pl.DeviceIdType.MESH,
        )

    own = [own_copy(i, own_sem.at[i]) for i in range(count)]
    own.append(pltpu.make_async_copy(x_ref, x_place, own_sem.at[count]))
    for index in range(count):
        hop(index, 0, True).start()
        hop(index, 0, False).start()
    for step in range(1, n_row):
        x_copy(step).start()
    for copy in own:
        copy.start()
    for step in range(half_way):
        for index in range(count):
            for to_right in (True, False):
                hop(index, step, to_right).wait_recv()
                if step + 1 < half_way:
                    hop(index, step + 1, to_right).start()
    for step in range(half_way):
        for index in range(count):
            for to_right in (True, False):
                hop(index, step, to_right).wait_send()
    for step in range(1, n_row):
        x_copy(step).wait()
    for copy in own:
        copy.wait()


def gather_all(layer_input, shards, by_rows):
    n_col, n_row = lax.axis_size("col"), lax.axis_size("row")
    count = len(shards)
    half_way = n_col // 2
    shapes = [
        jax.ShapeDtypeStruct((layer_input.shape[0], layer_input.shape[1] * n_row), jnp.bfloat16)
    ] + [
        jax.ShapeDtypeStruct(whole_shape(shard, rows, n_col), jnp.bfloat16)
        for shard, rows in zip(shards, by_rows)
    ]
    return pl.pallas_call(
        functools.partial(gather_kernel, by_rows, n_col, n_row),
        out_shape=shapes,
        in_specs=[pl.BlockSpec(memory_space=pl.ANY)] * (1 + count),
        out_specs=[pl.BlockSpec(memory_space=pl.ANY)] * (1 + count),
        scratch_shapes=[
            pltpu.SemaphoreType.DMA((count + 1,)),
            pltpu.SemaphoreType.DMA((n_row,)),
            pltpu.SemaphoreType.DMA((n_row,)),
        ]
        + [pltpu.SemaphoreType.DMA((count, half_way))] * 4,
        compiler_params=pltpu.CompilerParams(collective_id=0, has_side_effects=True),
        cost_estimate=pl.CostEstimate(
            flops=0, bytes_accessed=80_000_000, transcendentals=0
        ),
        name="gather_all",
    )(layer_input, *shards)


NT = (((1,), (1,)), ((), ()))


def columns_of(ref, index, width):
    if len(ref.shape) == 3:
        each = width // ref.shape[2]
        return jnp.concatenate([ref[index * each + i] for i in range(each)], axis=1)
    return ref[:, pl.ds(pl.multiple_of(index * width, 128), width)]


def layer_kernel(dims, *refs):
    n_col, n_row, heads, dec_count, page_count, score_scale, tail_shifts = dims
    (
        bias_ref,
        q_ref,
        k_ref,
        v_ref,
        var_col,
        var_row,
        keep_row,
        ask_ref,
        facts_ref,
        slot_bias,
        page_var,
        pool_ref,
        pick_ref,
        own_ref,
        x_ref,
        norm_ref,
        wo_ref,
        wg_shard,
        wu_shard,
        wd_shard,
        tail_ref,
        hidden_ref,
        tail_out,
        wg_ref,
        wu_ref,
        wd_ref,
        asked,
        answer,
        answered,
        attended,
        pair_send,
        pair_recv,
        sum_send,
        sum_recv,
        resid_all,
        normed,
        units,
        resid,
        own_sem,
        ask_send,
        ask_recv,
        ans_send,
        ans_recv,
        t_send,
        t_recv,
        pair_send_sem,
        pair_recv_sem,
        sum_send_sem,
        sum_recv_sem,
        far_send_sem,
        far_recv_sem,
        near_send_sem,
        near_recv_sem,
        r_send,
        r_recv,
        l_send,
        l_recv,
    ) = refs
    me, my_row = lax.axis_index("col"), lax.axis_index("row")
    half_way = n_col // 2
    rows, width = x_ref.shape
    pre_len = rows - dec_count
    greet(n_col, n_row)
    hop, own_copy = ring_hops(
        (True, True, False),
        n_col,
        (wg_shard, wu_shard, wd_shard),
        (wg_ref, wu_ref, wd_ref),
        (r_send, r_recv, l_send, l_recv),
    )

    def to_peer(src, dst, send, recv, step):
        return pltpu.make_async_remote_copy(
            src_ref=src,
            dst_ref=dst,
            send_sem=send.at[step],
            recv_sem=recv.at[step],
            device_id={"col": (me + step) % n_col},
            device_id_type=pl.DeviceIdType.MESH,
        )

    def ask(step):
        return to_peer(
            ask_ref.at[(me + step) % n_col], asked.at[me], ask_send, ask_recv, step
        )

    def reply(step):
        return to_peer(
            answer.at[(me + step) % n_col], answered.at[me], ans_send, ans_recv, step
        )

    def tail(at):
        return pltpu.make_async_remote_copy(
            src_ref=tail_ref.at[at],
            dst_ref=tail_out.at[at],
            send_sem=t_send.at[at],
            recv_sem=t_recv.at[at],
            device_id={"col": (me + tail_shifts[at]) % n_col},
            device_id_type=pl.DeviceIdType.MESH,
        )

    chips = n_row // 2
    chip, core = my_row // 2, my_row % 2

    def to_row(src, dst, send, recv, target):
        return pltpu.make_async_remote_copy(
            src_ref=src,
            dst_ref=dst,
            send_sem=send,
            recv_sem=recv,
            device_id={"row": target},
            device_id_type=pl.DeviceIdType.MESH,
        )

    def chip_at(step):
        return (chip + step) % chips

    def pair(stage, step):
        there = chip_at(step)
        return to_row(
            pair_send.at[stage, there],
            pair_recv.at[stage, there],
            pair_send_sem.at[stage, step],
            pair_recv_sem.at[stage, step],
            chip * 2 + 1 - core,
        )

    def summed(stage, step):
        there = chip_at(step)
        return to_row(
            sum_send.at[stage, there],
            sum_recv.at[stage, chip],
            sum_send_sem.at[stage, step],
            sum_recv_sem.at[stage, step],
            there * 2 + core,
        )

    def far(step):
        return to_row(
            resid_all.at[my_row],
            resid_all.at[my_row],
            far_send_sem.at[step],
            far_recv_sem.at[step],
            chip_at(step) * 2 + core,
        )

    def near(step):
        held = ((chip + chips - step) % chips) * 2 + core
        return to_row(
            resid_all.at[held],
            resid_all.at[held],
            near_send_sem.at[step],
            near_recv_sem.at[step],
            chip * 2 + 1 - core,
        )

    def reduce_start(stage, left, weight):
        def product(target):
            return jnp.dot(
                left[...], columns_of(weight, target, width), preferred_element_type=jnp.float32
            )

        steps = tuple(range(1, chips)) + (0,)
        for step in steps:
            there = chip_at(step)
            pair_send[stage, there] = product(there * 2 + 1 - core).astype(jnp.bfloat16)
            pair(stage, step).start()
        for step in steps:
            there = chip_at(step)
            mine = product(there * 2 + core)
            pair(stage, step).wait_recv()
            mine = mine + pair_recv[stage, there].astype(jnp.float32)
            if step == 0:
                return mine
            sum_send[stage, there] = mine.astype(jnp.bfloat16)
            summed(stage, step).start()

    def reduce_end(stage, total_share):
        for step in range(1, chips):
            summed(stage, step).wait_recv()
            there = (chip + chips - step) % chips
            total_share = total_share + sum_recv[stage, there].astype(jnp.float32)
        return total_share

    def pump(step):
        for index in range(3):
            for to_right in (True, False):
                hop(index, step, to_right).wait_recv()
                if step + 1 < half_way:
                    hop(index, step + 1, to_right).start()

    own_ask = pltpu.make_async_copy(ask_ref.at[me], asked.at[me], own_sem.at[3])
    for step in range(1, n_col):
        ask(step).start()
    own_ask.start()
    for index in range(3):
        hop(index, 0, True).start()
        hop(index, 0, False).start()
    for index in range(3):
        own_copy(index, own_sem.at[index]).start()

    block = 128
    lane_head = lax.broadcasted_iota(jnp.int32, (block, width), 1) // HD

    @pl.loop(0, pre_len // block)
    def _(at):
        start = pl.multiple_of(at * block, block)
        queries = q_ref[pl.ds(start, block), :]
        same = var_col[pl.ds(start, block), :] == var_row[...]
        query_at = lax.broadcasted_iota(jnp.int32, (block, pre_len), 0) + start
        key_at = lax.broadcasted_iota(jnp.int32, (block, pre_len), 1)
        allowed = (keep_row[...] == 1) | (query_at == key_at)
        result = jnp.zeros((block, width), jnp.float32)
        for head in range(heads):
            one = jnp.where(lane_head == head, queries.astype(jnp.float32), 0.0)
            scores = lax.dot_general(
                one.astype(jnp.bfloat16),
                k_ref[0:pre_len, :],
                NT,
                preferred_element_type=jnp.float32,
            )
            scores = scores * score_scale + jnp.where(same, bias_ref[0, head], bias_ref[1, head])
            weights = jnp.where(allowed, jnp.exp(scores), 0.0)
            weights = weights / jnp.sum(weights, axis=1, keepdims=True)
            mixed = jnp.dot(
                weights.astype(jnp.bfloat16),
                v_ref[0:pre_len, :],
                preferred_element_type=jnp.float32,
            )
            result = jnp.where(lane_head == head, mixed, result)
        attended[pl.ds(start, block), :] = result.astype(jnp.bfloat16)

    own_ask.wait()
    for step in range(1, n_col):
        ask(step).wait_recv()
    slots, page_size = asked.shape[0] * asked.shape[1], pool_ref.shape[2]
    queries = asked[...].reshape(slots, width).astype(jnp.bfloat16)
    facts = facts_ref[...]
    length = facts[:, page_count : page_count + 1]
    variate = facts[:, page_count + 1 : page_count + 2]
    same_bias, diff_bias = slot_bias[:, 0:1], slot_bias[:, 1:2]
    row_at = lax.broadcasted_iota(jnp.int32, (slots, page_size), 1)

    def one_page(page, carry):
        acc, total = carry
        scores = lax.dot_general(
            queries, pool_ref[page, 0], NT, preferred_element_type=jnp.float32
        )
        same = page_var[pl.ds(page, 1), :] == variate
        scores = scores * score_scale + jnp.where(same, same_bias, diff_bias)
        used = jnp.zeros((slots, page_size), jnp.float32)
        for entry in range(page_count):
            left_over = jnp.where(
                facts[:, entry : entry + 1] == page, length - entry * page_size, 0
            )
            used = used + jnp.where(row_at < left_over, 1.0, 0.0)
        weights = jnp.where(used > 0.0, used * jnp.exp(scores), 0.0)
        total = total + jnp.sum(weights, axis=1, keepdims=True)
        acc = acc + jnp.dot(
            weights.astype(jnp.bfloat16), pool_ref[page, 1], preferred_element_type=jnp.float32
        )
        return acc, total

    acc, total = lax.fori_loop(
        0,
        pool_ref.shape[0],
        one_page,
        (jnp.zeros((slots, width), jnp.float32), jnp.zeros((slots, 1), jnp.float32)),
    )
    mean = jnp.where(total > 0.0, acc / jnp.where(total > 0.0, total, 1.0), 0.0)
    answer[:, :, 0:width] = mean.reshape(n_col, slots // n_col, width)
    answer[:, :, width:] = jnp.broadcast_to(total, (slots, 128)).reshape(
        n_col, slots // n_col, 128
    )
    own_reply = pltpu.make_async_copy(answer.at[me], answered.at[me], own_sem.at[5])
    own_reply.start()
    for step in range(1, n_col):
        reply(step).start()
    pump(0)
    own_reply.wait()
    for step in range(1, n_col):
        reply(step).wait_recv()
    back = answered[...].reshape(slots, width + 128)
    slot_head = (lax.broadcasted_iota(jnp.int32, (slots, width), 0) % (slots // n_col)) % heads
    mine = lax.broadcasted_iota(jnp.int32, (slots, width), 1) // HD == slot_head
    pick = pick_ref[...]
    cached = jnp.dot(
        pick,
        jnp.where(mine, back[:, 0:width], 0.0),
        preferred_element_type=jnp.float32,
        precision=lax.Precision.HIGHEST,
    )
    cached_total = jnp.dot(
        pick,
        jnp.where(mine, jnp.broadcast_to(back[:, width : width + 1], (slots, width)), 0.0),
        preferred_element_type=jnp.float32,
        precision=lax.Precision.HIGHEST,
    )
    own_exp = own_ref[...]
    whole_total = cached_total + own_exp
    attended[pl.ds(pre_len, dec_count), :] = (
        cached * (cached_total / whole_total)
        + v_ref[pre_len:rows, :].astype(jnp.float32) * (own_exp / whole_total)
    ).astype(jnp.bfloat16)

    resid[...] = reduce_start(0, attended, wo_ref) + x_ref[...].astype(jnp.float32)
    pump(1)
    total_share = reduce_end(0, resid[...])
    resid[...] = total_share
    resid_all[my_row] = total_share.astype(jnp.bfloat16)
    for step in range(1, chips):
        far(step).start()
    near(0).start()
    for step in range(2, half_way):
        pump(step)
    for at in range(len(tail_shifts)):
        tail(at).start()
    for step in range(1, chips):
        far(step).wait_recv()
        near(step).start()
    for step in range(chips):
        near(step).wait_recv()
    squares = jnp.zeros((rows, 1), jnp.float32)
    for piece in range(n_row):
        values = resid_all[piece].astype(jnp.float32)
        squares = squares + jnp.sum(values * values, axis=1, keepdims=True)
    scale = lax.rsqrt(squares * (1.0 / (n_row * width)) + eps)
    for piece in range(n_row):
        cols = slice(piece * width, (piece + 1) * width)
        normed[:, cols] = (
            resid_all[piece].astype(jnp.float32) * scale * norm_ref[:, cols]
        ).astype(jnp.bfloat16)
    for index in range(3):
        own_copy(index, own_sem.at[index]).wait()

    tile = 256

    @pl.loop(0, units.shape[1] // tile)
    def _(at):
        cols = pl.ds(pl.multiple_of(at * tile, tile), tile)
        gate = jnp.dot(normed[...], wg_ref[:, cols], preferred_element_type=jnp.float32)
        up = jnp.dot(normed[...], wu_ref[:, cols], preferred_element_type=jnp.float32)
        units[:, cols] = (gate / (1.0 + jnp.exp(-gate)) * up).astype(jnp.bfloat16)

    resid[...] = reduce_start(1, units, wd_ref) + resid[...]
    hidden_ref[...] = reduce_end(1, resid[...]).astype(jnp.bfloat16)

    for at in range(len(tail_shifts)):
        tail(at).wait()
    for step in range(chips):
        pair(0, step).wait_send()
        pair(1, step).wait_send()
        near(step).wait_send()
    for step in range(1, chips):
        summed(0, step).wait_send()
        summed(1, step).wait_send()
        far(step).wait_send()
    for step in range(1, n_col):
        ask(step).wait_send()
        reply(step).wait_send()
    for step in range(half_way):
        for index in range(3):
            for to_right in (True, False):
                hop(index, step, to_right).wait_send()


def rest_of_layer(dims, *operands):
    n_col, n_row = dims[:2]
    x, wg, wu, wd, tails = operands[14], operands[17], operands[18], operands[19], operands[20]
    ask = operands[7]
    rows, width = x.shape
    half_way = n_col // 2
    chips = n_row // 2
    full = n_row * width
    vmem = pl.BlockSpec(memory_space=pltpu.VMEM)
    anywhere = pl.BlockSpec(memory_space=pl.ANY)
    dma = pltpu.SemaphoreType.DMA
    return pl.pallas_call(
        functools.partial(layer_kernel, dims),
        out_shape=[
            jax.ShapeDtypeStruct((rows, width), jnp.bfloat16),
            jax.ShapeDtypeStruct(tails.shape, jnp.bfloat16),
        ],
        in_specs=[pl.BlockSpec(memory_space=pltpu.SMEM)] + [vmem] * 19 + [anywhere],
        out_specs=[vmem, anywhere],
        scratch_shapes=[
            pltpu.VMEM(whole_shape(wg, True, n_col), jnp.bfloat16),
            pltpu.VMEM(whole_shape(wu, True, n_col), jnp.bfloat16),
            pltpu.VMEM(whole_shape(wd, False, n_col), jnp.bfloat16),
            pltpu.VMEM(ask.shape, jnp.float32),
            pltpu.VMEM(ask.shape[:2] + (width + 128,), jnp.float32),
            pltpu.VMEM(ask.shape[:2] + (width + 128,), jnp.float32),
            pltpu.VMEM((rows, width), jnp.bfloat16),
            pltpu.VMEM((2, chips, rows, width), jnp.bfloat16),
            pltpu.VMEM((2, chips, rows, width), jnp.bfloat16),
            pltpu.VMEM((2, chips, rows, width), jnp.bfloat16),
            pltpu.VMEM((2, chips, rows, width), jnp.bfloat16),
            pltpu.VMEM((n_row, rows, width), jnp.bfloat16),
            pltpu.VMEM((rows, full), jnp.bfloat16),
            pltpu.VMEM((rows, wg.shape[1]), jnp.bfloat16),
            pltpu.VMEM((rows, width), jnp.float32),
            dma((6,)),
        ]
        + [dma((n_col,))] * 4
        + [dma((tails.shape[0],))] * 2
        + [dma((2, chips))] * 4
        + [dma((chips,))] * 4
        + [dma((3, half_way))] * 4,
        compiler_params=pltpu.CompilerParams(
            collective_id=1, has_side_effects=True, vmem_limit_bytes=50 * 1024 * 1024
        ),
        cost_estimate=pl.CostEstimate(
            flops=200_000_000_000, bytes_accessed=200_000_000, transcendentals=2_000_000
        ),
        name="rest_of_layer",
    )(*operands)


def on_device(
    layer_input,
    w_q,
    w_k,
    w_v,
    w_o,
    w_gate,
    w_up,
    w_down,
    norm1,
    norm2,
    q_gain,
    k_gain,
    bias_same,
    bias_diff,
    pre_variate,
    pre_keep,
    dec_variate,
    dec_len,
    dec_table,
    dec_holder,
    kv_pool,
    page_variates,
):
    row_count = layer_input.shape[0]
    local_width = layer_input.shape[1]
    pre_len = pre_variate.shape[1]
    dec_count = dec_len.shape[0]
    heads_here = local_width // HD
    score_scale = HD ** (-0.5)
    page_size = kv_pool.shape[2]
    page_count = dec_table.shape[1]
    peer_count = lax.axis_size("col")
    slot_count = max(2, (dec_count + peer_count - 1) // peer_count)
    holder = dec_holder[:, 0]
    onehot = (holder[:, None] == jnp.arange(peer_count)[None, :]).astype(jnp.int32)
    slot_rank = jnp.sum((jnp.cumsum(onehot, axis=0) - onehot) * onehot, axis=1)
    target = holder * slot_count + slot_rank
    int_facts = jnp.concatenate([dec_table, dec_len[:, None], dec_variate[:, None]], axis=1)
    all_slots = peer_count * slot_count
    to_slot = target[None, :] == jnp.arange(all_slots)[:, None]
    send_int = jnp.sum(jnp.where(to_slot[:, :, None], int_facts[None], 0), axis=1)
    send_int = send_int.reshape(peer_count, slot_count, page_count + 2)
    int_part = lax.all_to_all(send_int, "col", split_axis=0, concat_axis=0, tiled=True)
    slot_ints = int_part.reshape(all_slots, page_count + 2)
    slot_table = slot_ints[:, :page_count]
    slot_len = slot_ints[:, page_count]
    slot_variate = slot_ints[:, page_count + 1]
    last_place = (slot_len // page_size)[:, None] == jnp.arange(page_count)[None, :]
    last_page = jnp.sum(jnp.where(last_place, slot_table, 0), axis=1)
    my_col = lax.axis_index("col")
    shift_peer = (my_col + jnp.arange(peer_count)) % peer_count
    tail_send = kv_pool[last_page.reshape(peer_count, slot_count)[shift_peer].reshape(-1)]
    tail_send = tail_send.reshape(peer_count, slot_count, 2, page_size, local_width)
    first_shift = max(peer_count // 2 - 2, 1)
    last_shift = min(first_shift + 5, peer_count)
    kernel_shifts = tuple(range(1, first_shift)) + tuple(range(last_shift, peer_count))
    tail_parts = {0: tail_send[0]}
    for shift in range(first_shift, last_shift):
        tail_parts[shift] = lax.ppermute(
            tail_send[shift],
            "col",
            [(source, (source + shift) % peer_count) for source in range(peer_count)],
        )
    kernel_tails = jnp.stack([tail_send[shift] for shift in kernel_shifts])
    gathered_input, full_q, full_k, full_v, full_o = gather_all(
        layer_input, (w_q, w_k, w_v, w_o), (True, True, True, False)
    )
    normed = norm_rows(gathered_input.astype(jnp.float32), norm1).astype(jnp.bfloat16)
    queries = jnp.dot(normed, full_q, preferred_element_type=jnp.float32)
    keys_proj = jnp.dot(normed, full_k, preferred_element_type=jnp.float32)
    values_proj = jnp.dot(normed, full_v, preferred_element_type=jnp.float32)
    places = jnp.concatenate([segment_time(pre_variate[0]), dec_len])
    query_rot = rotate(
        norm_rows(queries.reshape(row_count, heads_here, HD), q_gain.reshape(heads_here, HD)),
        places,
    ).astype(jnp.bfloat16)
    key_rot = rotate(
        norm_rows(keys_proj.reshape(row_count, heads_here, HD), k_gain.reshape(heads_here, HD)),
        places,
    ).astype(jnp.bfloat16)
    value_bf = values_proj.astype(jnp.bfloat16).reshape(row_count, heads_here, HD)

    flat_query = query_rot.reshape(row_count, local_width)
    flat_key = key_rot.reshape(row_count, local_width)
    flat_value = value_bf.reshape(row_count, local_width)

    used_rows = slot_count * heads_here
    slot_rows = -(-used_rows // 8) * 8
    sent_query = jnp.dot(
        to_slot.astype(jnp.bfloat16), flat_query[pre_len:], preferred_element_type=jnp.float32
    )
    lane_head = jnp.arange(local_width) // HD
    head_rows = (jnp.arange(heads_here)[:, None] == lane_head[None, :]).astype(jnp.float32)
    ask = (sent_query[:, None, :] * head_rows[None]).reshape(peer_count, used_rows, local_width)
    ask = jnp.pad(ask, ((0, 0), (0, slot_rows - used_rows), (0, 0)))

    def per_row(values):
        wide = jnp.broadcast_to(
            values.reshape(peer_count, slot_count, 1, -1),
            (peer_count, slot_count, heads_here, values.shape[-1]),
        ).reshape(peer_count, used_rows, -1)
        wide = jnp.pad(wide, ((0, 0), (0, slot_rows - used_rows), (0, 0)))
        return wide.reshape(peer_count * slot_rows, -1)

    facts = per_row(slot_ints)
    bias_pair = jnp.stack([bias_same, bias_diff], axis=1)
    slot_bias = jnp.tile(
        jnp.pad(jnp.tile(bias_pair, (slot_count, 1)), ((0, slot_rows - used_rows), (0, 0))),
        (peer_count, 1),
    )
    pick = per_row(to_slot.astype(jnp.float32)).T
    own_score = (
        jnp.sum(
            query_rot[pre_len:].astype(jnp.float32) * key_rot[pre_len:].astype(jnp.float32), axis=2
        )
        * score_scale
        + bias_same[None]
    )
    own_exp = jnp.repeat(jnp.exp(own_score), HD, axis=1)
    hidden, tail_back = rest_of_layer(
        (
            peer_count,
            lax.axis_size("row"),
            heads_here,
            dec_count,
            page_count,
            score_scale,
            kernel_shifts,
        ),
        jnp.stack([bias_same, bias_diff]),
        flat_query,
        flat_key,
        flat_value,
        pre_variate[0][:, None],
        pre_variate,
        pre_keep,
        ask,
        facts,
        slot_bias,
        page_variates,
        kv_pool,
        pick,
        own_exp,
        layer_input,
        norm2[None],
        full_o,
        w_gate,
        w_up,
        w_down,
        kernel_tails,
    )
    for at, shift in enumerate(kernel_shifts):
        tail_parts[shift] = tail_back[at]
    tail_at = ((my_col - holder) % peer_count) * slot_count + slot_rank
    old_tails = jnp.concatenate([tail_parts[i] for i in range(peer_count)], axis=0)[tail_at]
    hit_row = (jnp.arange(page_size)[None, :] == (dec_len % page_size)[:, None])[:, None, :, None]
    new_rows = jnp.stack([flat_key[pre_len:], flat_value[pre_len:]], axis=1)[:, :, None, :]
    tail_pages = jnp.where(hit_row, new_rows, old_tails)
    prefill_pages = jnp.stack(
        [
            key_rot[:pre_len].reshape(pre_len // page_size, page_size, local_width),
            value_bf[:pre_len].reshape(pre_len // page_size, page_size, local_width),
        ],
        axis=1,
    )
    return (hidden, prefill_pages, tail_pages)


def solution(mesh):
    placed = (
        P("col", "row"),
        P("col", "row"),
        P("col", "row"),
        P("col", "row"),
        P("row", "col"),
        P("col", "row"),
        P("col", "row"),
        P("row", "col"),
        P(),
        P(),
        P("row"),
        P("row"),
        P("row"),
        P("row"),
        P("col", None),
        P("col", None),
        P("col"),
        P("col"),
        P("col", None),
        P("col", None),
        P("col", None, None, "row"),
        P("col", None),
    )
    return jax.shard_map(
        on_device,
        mesh=mesh,
        in_specs=placed,
        out_specs=(P("col", "row"), P("col", None, None, "row"), P("col", None, None, "row")),
        check_vma=False,
    )
```

```python
import functools

import jax
import jax.numpy as jnp
from jax import lax
from jax.experimental import pallas as pl
from jax.experimental.pallas import tpu as pltpu
from jax.sharding import PartitionSpec as P

HD = 64


eps = 1e-05


def segment_time(variates):
    places = jnp.arange(variates.shape[0])
    run_start = jnp.concatenate([jnp.ones((1,), dtype=jnp.bool_), variates[1:] != variates[:-1]])
    starts = lax.cummax(jnp.where(run_start, places, 0), axis=0)
    return places - starts


def cycle_dims(count):
    inner = 1
    while inner * inner * 4 <= count:
        inner *= 2
    return count // inner, inner


def cycle_place(member, count):
    outer, inner = cycle_dims(count)
    if inner == 1:
        return member
    z, y = member // inner, member % inner
    back = outer - 1 - z
    odd = back % 2
    along = (1 - odd) * (y - 1) + odd * (inner - 1 - y)
    return jnp.where(y == 0, z, outer + back * (inner - 1) + along)


def cycle_member(place, count):
    outer, inner = cycle_dims(count)
    if inner == 1:
        return place
    rest = jnp.maximum(place - outer, 0)
    back, along = rest // (inner - 1), rest % (inner - 1)
    odd = back % 2
    y = (1 - odd) * (1 + along) + odd * (inner - 1 - along)
    return jnp.where(place < outer, place * inner, (outer - 1 - back) * inner + y)


def greet(n_col, n_row):
    me, my_row = lax.axis_index("col"), lax.axis_index("row")
    barrier = pltpu.get_barrier_semaphore()
    for step in range(1, n_col):
        pl.semaphore_signal(
            barrier,
            inc=1,
            device_id={"col": (me + step) % n_col},
            device_id_type=pl.DeviceIdType.MESH,
        )
    for step in range(1, n_row):
        pl.semaphore_signal(
            barrier,
            inc=1,
            device_id={"row": (my_row + step) % n_row},
            device_id_type=pl.DeviceIdType.MESH,
        )
    pl.semaphore_wait(barrier, n_col + n_row - 2)


def ring_hops(by_rows, n_col, shards, wholes, sems):
    me = lax.axis_index("col")
    place = cycle_place(me, n_col)
    right = cycle_member((place + 1) % n_col, n_col)
    left = cycle_member((place + n_col - 1) % n_col, n_col)
    half_way = n_col // 2
    r_send, r_recv, l_send, l_recv = sems

    def part(index, owner, low, size):
        shard, ref = shards[index], wholes[index]
        if by_rows[index]:
            depth = shard.shape[0]
            start = pl.multiple_of(owner * depth + low, 16)
            return ref.at[pl.ds(start, size)]
        width = shard.shape[1]
        if width % 128:
            return ref.at[owner, pl.ds(low, size)]
        return ref.at[pl.ds(low, size), pl.ds(pl.multiple_of(owner * width, 128), width)]

    def hop(index, step, to_right):
        shift = n_col - step if to_right else step
        owner = cycle_member((place + shift) % n_col, n_col)
        depth = shards[index].shape[0]
        low, size = 0, depth
        if step == half_way - 1:
            low, size = (0, depth // 2) if to_right else (depth // 2, depth // 2)
        there = part(index, owner, low, size)
        here = shards[index].at[pl.ds(low, size)] if step == 0 else there
        send, recv = (r_send, r_recv) if to_right else (l_send, l_recv)
        return pltpu.make_async_remote_copy(
            src_ref=here,
            dst_ref=there,
            send_sem=send.at[index, step],
            recv_sem=recv.at[index, step],
            device_id={"col": right if to_right else left},
            device_id_type=pl.DeviceIdType.MESH,
        )

    def own_copy(index, sem):
        return pltpu.make_async_copy(
            shards[index], part(index, me, 0, shards[index].shape[0]), sem
        )

    return hop, own_copy


def whole_shape(shard, rows, n_col):
    depth, width = shard.shape
    if rows:
        return (depth * n_col, width)
    if width % 128:
        return (n_col, depth, width)
    return (depth, width * n_col)


NT = (((1,), (1,)), ((), ()))


def columns_of(ref, index, width):
    if len(ref.shape) == 3:
        each = width // ref.shape[2]
        return jnp.concatenate([ref[index * each + i] for i in range(each)], axis=1)
    return ref[:, pl.ds(pl.multiple_of(index * width, 128), width)]


def layer_kernel(dims, *refs):
    n_col, n_row, heads, dec_count, page_count, score_scale, slot_count = dims
    (
        bias_ref,
        page_ref,
        var_col,
        var_row,
        keep_row,
        facts_ref,
        slot_bias,
        lane_bias,
        page_var,
        pick_ref,
        place_ref,
        cos_ref,
        sin_ref,
        gain_ref,
        norm_ref,
        x_ref,
        pool_hbm,
        wq_shard,
        wk_shard,
        wv_shard,
        wo_shard,
        wg_shard,
        wu_shard,
        wd_shard,
        hidden_ref,
        k_ref,
        v_ref,
        tail_out,
        wq_ref,
        wk_ref,
        wv_ref,
        wo_ref,
        wg_ref,
        wu_ref,
        wd_ref,
        pool_ref,
        tail_ref,
        q_ref,
        ask_ref,
        asked,
        answer,
        answered,
        attended,
        pair_send,
        pair_recv,
        sum_send,
        sum_recv,
        x_all,
        resid_all,
        normed,
        units,
        resid,
        own_sem,
        ask_send,
        ask_recv,
        ans_send,
        ans_recv,
        t_send,
        t_recv,
        pair_send_sem,
        pair_recv_sem,
        sum_send_sem,
        sum_recv_sem,
        far_send_sem,
        far_recv_sem,
        near_send_sem,
        near_recv_sem,
        r_send,
        r_recv,
        l_send,
        l_recv,
    ) = refs
    me, my_row = lax.axis_index("col"), lax.axis_index("row")
    half_way = n_col // 2
    rows, width = x_ref.shape
    pre_len = rows - dec_count
    greet(n_col, n_row)
    hop, own_copy = ring_hops(
        (True, True, True, False, True, True, False),
        n_col,
        (wq_shard, wk_shard, wv_shard, wo_shard, wg_shard, wu_shard, wd_shard),
        (wq_ref, wk_ref, wv_ref, wo_ref, wg_ref, wu_ref, wd_ref),
        (r_send, r_recv, l_send, l_recv),
    )

    def to_peer(src, dst, send, recv, step):
        return pltpu.make_async_remote_copy(
            src_ref=src,
            dst_ref=dst,
            send_sem=send.at[step],
            recv_sem=recv.at[step],
            device_id={"col": (me + step) % n_col},
            device_id_type=pl.DeviceIdType.MESH,
        )

    def ask(step):
        return to_peer(
            ask_ref.at[(me + step) % n_col], asked.at[me], ask_send, ask_recv, step
        )

    def reply(step):
        return to_peer(
            answer.at[(me + step) % n_col], answered.at[me], ans_send, ans_recv, step
        )

    def tail(step):
        return to_peer(tail_ref.at[step], tail_out.at[step], t_send, t_recv, step)

    chips = n_row // 2
    chip, core = my_row // 2, my_row % 2

    def to_row(src, dst, send, recv, target):
        return pltpu.make_async_remote_copy(
            src_ref=src,
            dst_ref=dst,
            send_sem=send,
            recv_sem=recv,
            device_id={"row": target},
            device_id_type=pl.DeviceIdType.MESH,
        )

    def chip_at(step):
        return (chip + step) % chips

    def pair(stage, step):
        there = chip_at(step)
        return to_row(
            pair_send.at[stage, there],
            pair_recv.at[stage, there],
            pair_send_sem.at[stage, step],
            pair_recv_sem.at[stage, step],
            chip * 2 + 1 - core,
        )

    def summed(stage, step):
        there = chip_at(step)
        return to_row(
            sum_send.at[stage, there],
            sum_recv.at[stage, chip],
            sum_send_sem.at[stage, step],
            sum_recv_sem.at[stage, step],
            there * 2 + core,
        )

    def far(stage, step):
        held = (x_all, resid_all)[stage].at[my_row]
        return to_row(
            held,
            held,
            far_send_sem.at[stage, step],
            far_recv_sem.at[stage, step],
            chip_at(step) * 2 + core,
        )

    def near(stage, step):
        held = (x_all, resid_all)[stage].at[((chip + chips - step) % chips) * 2 + core]
        return to_row(
            held,
            held,
            near_send_sem.at[stage, step],
            near_recv_sem.at[stage, step],
            chip * 2 + 1 - core,
        )

    def share_start(stage):
        for step in range(1, chips):
            far(stage, step).start()
        near(stage, 0).start()

    def share_end(stage):
        for step in range(1, chips):
            far(stage, step).wait_recv()
            near(stage, step).start()
        for step in range(chips):
            near(stage, step).wait_recv()

    def norm_all(held, which):
        squares = jnp.zeros((rows, 1), jnp.float32)
        for piece in range(n_row):
            values = held[piece].astype(jnp.float32)
            squares = squares + jnp.sum(values * values, axis=1, keepdims=True)
        scale = lax.rsqrt(squares * (1.0 / (n_row * width)) + eps)
        for piece in range(n_row):
            cols = slice(piece * width, (piece + 1) * width)
            normed[:, cols] = (
                held[piece].astype(jnp.float32) * scale * norm_ref[which : which + 1, cols]
            ).astype(jnp.bfloat16)

    def reduce_start(stage, left, weight):
        def product(target):
            return jnp.dot(
                left[...], columns_of(weight, target, width), preferred_element_type=jnp.float32
            )

        steps = tuple(range(1, chips)) + (0,)
        for step in steps:
            there = chip_at(step)
            pair_send[stage, there] = product(there * 2 + 1 - core).astype(jnp.bfloat16)
            pair(stage, step).start()
        for step in steps:
            there = chip_at(step)
            mine = product(there * 2 + core)
            pair(stage, step).wait_recv()
            mine = mine + pair_recv[stage, there].astype(jnp.float32)
            if step == 0:
                return mine
            sum_send[stage, there] = mine.astype(jnp.bfloat16)
            summed(stage, step).start()

    def reduce_end(stage, total_share):
        for step in range(1, chips):
            summed(stage, step).wait_recv()
            there = (chip + chips - step) % chips
            total_share = total_share + sum_recv[stage, there].astype(jnp.float32)
        return total_share

    early, late = (0, 1, 2), (3, 4, 5, 6)

    def begin(index):
        hop(index, 0, True).start()
        hop(index, 0, False).start()
        own_copy(index, own_sem.at[index]).start()

    def pump(group, step):
        for index in group:
            for to_right in (True, False):
                hop(index, step, to_right).wait_recv()
                if step + 1 < half_way:
                    hop(index, step + 1, to_right).start()

    own_ask = pltpu.make_async_copy(ask_ref.at[me], asked.at[me], own_sem.at[7])
    own_tail = pltpu.make_async_copy(tail_ref.at[0], tail_out.at[0], own_sem.at[8])
    pool_copy = pltpu.make_async_copy(pool_hbm, pool_ref, own_sem.at[10])
    for index in early:
        begin(index)
    x_all[my_row] = x_ref[...]
    share_start(0)
    pool_copy.start()
    pump(early, 0)
    begin(3)
    begin(4)
    share_end(0)
    norm_all(x_all, 0)
    pump(early, 1)
    pool_copy.wait()
    for step in range(n_col):
        for slot in range(slot_count):
            tail_ref[step, slot] = pool_ref[page_ref[step * slot_count + slot]]
    begin(5)
    begin(6)
    for step in range(2, half_way):
        pump(early, step)
    for index in early:
        own_copy(index, own_sem.at[index]).wait()

    row_lane = lax.broadcasted_iota(jnp.int32, (width, width), 0)
    col_lane = lax.broadcasted_iota(jnp.int32, (width, width), 1)
    same_head = jnp.where(row_lane // HD == col_lane // HD, 1.0, 0.0)
    upper = col_lane % HD >= HD // 2
    turn = jnp.where(upper & (row_lane == col_lane - HD // 2), 1.0, 0.0) - jnp.where(
        jnp.logical_not(upper) & (row_lane == col_lane + HD // 2), 1.0, 0.0
    )

    def exact(left, right):
        return jnp.dot(
            left, right, preferred_element_type=jnp.float32, precision=lax.Precision.HIGHEST
        )

    def rotated(weight, which):
        value = jnp.dot(normed[...], weight[...], preferred_element_type=jnp.float32)
        square = exact(value * value, same_head) * (1.0 / HD)
        value = value * lax.rsqrt(square + eps) * gain_ref[which : which + 1, :]
        return (value * cos_ref[...] + exact(value, turn) * sin_ref[...]).astype(jnp.bfloat16)

    q_ref[...] = rotated(wq_ref, 0)
    slots, page_size = asked.shape[0] * asked.shape[1], pool_ref.shape[2]
    slot_head = (lax.broadcasted_iota(jnp.int32, (slots, width), 0) % (slots // n_col)) % heads
    mine = lax.broadcasted_iota(jnp.int32, (slots, width), 1) // HD == slot_head
    sent = jnp.dot(place_ref[...], q_ref[pre_len:rows, :], preferred_element_type=jnp.float32)
    ask_ref[...] = jnp.where(mine, sent, 0.0).reshape(n_col, slots // n_col, width)
    for step in range(1, n_col):
        ask(step).start()
    own_ask.start()
    own_tail.start()
    k_ref[...] = rotated(wk_ref, 1)
    v_ref[...] = jnp.dot(normed[...], wv_ref[...], preferred_element_type=jnp.float32).astype(
        jnp.bfloat16
    )
    pump(late, 0)
    tail(1).start()
    tail(n_col - 1).start()

    block = 128
    lane_head = lax.broadcasted_iota(jnp.int32, (block, width), 1) // HD

    @pl.loop(0, pre_len // block)
    def _(at):
        start = pl.multiple_of(at * block, block)
        queries = q_ref[pl.ds(start, block), :]
        same = var_col[pl.ds(start, block), :] == var_row[...]
        query_at = lax.broadcasted_iota(jnp.int32, (block, pre_len), 0) + start
        key_at = lax.broadcasted_iota(jnp.int32, (block, pre_len), 1)
        allowed = (keep_row[...] == 1) | (query_at == key_at)
        result = jnp.zeros((block, width), jnp.float32)
        for head in range(heads):
            one = jnp.where(lane_head == head, queries.astype(jnp.float32), 0.0)
            scores = lax.dot_general(
                one.astype(jnp.bfloat16),
                k_ref[0:pre_len, :],
                NT,
                preferred_element_type=jnp.float32,
            )
            scores = scores * score_scale + jnp.where(same, bias_ref[0, head], bias_ref[1, head])
            weights = jnp.where(allowed, jnp.exp(scores), 0.0)
            weights = weights / jnp.sum(weights, axis=1, keepdims=True)
            mixed = jnp.dot(
                weights.astype(jnp.bfloat16),
                v_ref[0:pre_len, :],
                preferred_element_type=jnp.float32,
            )
            result = jnp.where(lane_head == head, mixed, result)
        attended[pl.ds(start, block), :] = result.astype(jnp.bfloat16)

    own_ask.wait()
    for step in range(1, n_col):
        ask(step).wait_recv()
    queries = asked[...].reshape(slots, width).astype(jnp.bfloat16)
    facts = facts_ref[...]
    length = facts[:, page_count : page_count + 1]
    variate = facts[:, page_count + 1 : page_count + 2]
    same_bias, diff_bias = slot_bias[:, 0:1], slot_bias[:, 1:2]
    row_at = lax.broadcasted_iota(jnp.int32, (slots, page_size), 1)

    def one_page(page, carry):
        acc, total = carry
        scores = lax.dot_general(
            queries, pool_ref[page, 0], NT, preferred_element_type=jnp.float32
        )
        same = page_var[pl.ds(page, 1), :] == variate
        scores = scores * score_scale + jnp.where(same, same_bias, diff_bias)
        used = jnp.zeros((slots, page_size), jnp.float32)
        for entry in range(page_count):
            left_over = jnp.where(
                facts[:, entry : entry + 1] == page, length - entry * page_size, 0
            )
            used = used + jnp.where(row_at < left_over, 1.0, 0.0)
        weights = jnp.where(used > 0.0, used * jnp.exp(scores), 0.0)
        total = total + jnp.sum(weights, axis=1, keepdims=True)
        acc = acc + jnp.dot(
            weights.astype(jnp.bfloat16), pool_ref[page, 1], preferred_element_type=jnp.float32
        )
        return acc, total

    acc, total = lax.fori_loop(
        0,
        pool_ref.shape[0],
        one_page,
        (jnp.zeros((slots, width), jnp.float32), jnp.zeros((slots, 1), jnp.float32)),
    )
    mean = jnp.where(total > 0.0, acc / jnp.where(total > 0.0, total, 1.0), 0.0)
    answer[:, :, 0:width] = mean.reshape(n_col, slots // n_col, width)
    answer[:, :, width:] = jnp.broadcast_to(total, (slots, 128)).reshape(
        n_col, slots // n_col, 128
    )
    own_reply = pltpu.make_async_copy(answer.at[me], answered.at[me], own_sem.at[9])
    own_reply.start()
    for step in range(1, n_col):
        reply(step).start()
    pump(late, 1)
    if n_col > 4:
        tail(2).start()
        tail(n_col - 2).start()
    own_reply.wait()
    for step in range(1, n_col):
        reply(step).wait_recv()
    back = answered[...].reshape(slots, width + 128)
    pick = pick_ref[...]
    cached = jnp.dot(
        pick,
        jnp.where(mine, back[:, 0:width], 0.0),
        preferred_element_type=jnp.float32,
        precision=lax.Precision.HIGHEST,
    )
    cached_total = jnp.dot(
        pick,
        jnp.where(mine, jnp.broadcast_to(back[:, width : width + 1], (slots, width)), 0.0),
        preferred_element_type=jnp.float32,
        precision=lax.Precision.HIGHEST,
    )
    own_score = exact(
        q_ref[pre_len:rows, :].astype(jnp.float32) * k_ref[pre_len:rows, :].astype(jnp.float32),
        same_head,
    )
    own_exp = jnp.exp(own_score * score_scale + lane_bias[...])
    whole_total = cached_total + own_exp
    attended[pl.ds(pre_len, dec_count), :] = (
        cached * (cached_total / whole_total)
        + v_ref[pre_len:rows, :].astype(jnp.float32) * (own_exp / whole_total)
    ).astype(jnp.bfloat16)

    own_copy(3, own_sem.at[3]).wait()
    if half_way > 2:
        pump((3,), 2)
    for step in range(3, half_way):
        pump((3,), step)
    resid[...] = reduce_start(0, attended, wo_ref) + x_ref[...].astype(jnp.float32)
    if half_way > 2:
        pump(late[1:], 2)
    total_share = reduce_end(0, resid[...])
    resid[...] = total_share
    resid_all[my_row] = total_share.astype(jnp.bfloat16)
    share_start(1)
    for step in range(3, half_way):
        pump(late[1:], step)
    for step in range(3, n_col - 2):
        tail(step).start()
    share_end(1)
    norm_all(resid_all, 1)
    for index in late[1:]:
        own_copy(index, own_sem.at[index]).wait()

    tile = 256

    @pl.loop(0, units.shape[1] // tile)
    def _(at):
        cols = pl.ds(pl.multiple_of(at * tile, tile), tile)
        gate = jnp.dot(normed[...], wg_ref[:, cols], preferred_element_type=jnp.float32)
        up = jnp.dot(normed[...], wu_ref[:, cols], preferred_element_type=jnp.float32)
        units[:, cols] = (gate / (1.0 + jnp.exp(-gate)) * up).astype(jnp.bfloat16)

    resid[...] = reduce_start(1, units, wd_ref) + resid[...]
    hidden_ref[...] = reduce_end(1, resid[...]).astype(jnp.bfloat16)

    for step in range(chips):
        pair(0, step).wait_send()
        pair(1, step).wait_send()
        near(0, step).wait_send()
        near(1, step).wait_send()
    for step in range(1, chips):
        summed(0, step).wait_send()
        summed(1, step).wait_send()
        far(0, step).wait_send()
        far(1, step).wait_send()
    for step in range(1, n_col):
        ask(step).wait_send()
        reply(step).wait_send()
    for step in range(half_way):
        for index in range(7):
            for to_right in (True, False):
                hop(index, step, to_right).wait_send()
    own_tail.wait()
    for step in range(1, n_col):
        tail(step).wait()


def whole_layer(dims, operands, shards):
    n_col, n_row = dims[:2]
    slot_count = dims[6]
    x, pool = operands[15], operands[16]
    slot_rows = operands[5].shape[0] // n_col
    rows, width = x.shape
    half_way = n_col // 2
    chips = n_row // 2
    vmem = pl.BlockSpec(memory_space=pltpu.VMEM)
    smem = pl.BlockSpec(memory_space=pltpu.SMEM)
    anywhere = pl.BlockSpec(memory_space=pl.ANY)
    dma = pltpu.SemaphoreType.DMA
    tails = (n_col, slot_count) + pool.shape[1:]
    by_rows = (True, True, True, False, True, True, False)
    act = (rows, width)
    return pl.pallas_call(
        functools.partial(layer_kernel, dims),
        out_shape=[jax.ShapeDtypeStruct(act, jnp.bfloat16)] * 3
        + [jax.ShapeDtypeStruct(tails, jnp.bfloat16)],
        in_specs=[smem] * 2 + [vmem] * 14 + [anywhere] * 8,
        out_specs=[vmem] * 3 + [anywhere],
        scratch_shapes=[
            pltpu.VMEM(whole_shape(shard, along, n_col), jnp.bfloat16)
            for shard, along in zip(shards, by_rows)
        ]
        + [
            pltpu.VMEM(pool.shape, jnp.bfloat16),
            pltpu.VMEM(tails, jnp.bfloat16),
            pltpu.VMEM(act, jnp.bfloat16),
            pltpu.VMEM((n_col, slot_rows, width), jnp.float32),
            pltpu.VMEM((n_col, slot_rows, width), jnp.float32),
            pltpu.VMEM((n_col, slot_rows, width + 128), jnp.float32),
            pltpu.VMEM((n_col, slot_rows, width + 128), jnp.float32),
            pltpu.VMEM(act, jnp.bfloat16),
        ]
        + [pltpu.VMEM((2, chips) + act, jnp.bfloat16)] * 4
        + [pltpu.VMEM((n_row,) + act, jnp.bfloat16)] * 2
        + [
            pltpu.VMEM((rows, n_row * width), jnp.bfloat16),
            pltpu.VMEM((rows, shards[4].shape[1]), jnp.bfloat16),
            pltpu.VMEM(act, jnp.float32),
            dma((11,)),
        ]
        + [dma((n_col,))] * 6
        + [dma((2, chips))] * 8
        + [dma((7, half_way))] * 4,
        compiler_params=pltpu.CompilerParams(
            collective_id=0, has_side_effects=True, vmem_limit_bytes=56 * 1024 * 1024
        ),
        name="whole_layer",
    )(*operands, *shards)


def on_device(
    layer_input,
    w_q,
    w_k,
    w_v,
    w_o,
    w_gate,
    w_up,
    w_down,
    norm1,
    norm2,
    q_gain,
    k_gain,
    bias_same,
    bias_diff,
    pre_variate,
    pre_keep,
    dec_variate,
    dec_len,
    dec_table,
    dec_holder,
    kv_pool,
    page_variates,
):
    row_count = layer_input.shape[0]
    local_width = layer_input.shape[1]
    pre_len = pre_variate.shape[1]
    dec_count = dec_len.shape[0]
    heads_here = local_width // HD
    score_scale = HD ** (-0.5)
    page_size = kv_pool.shape[2]
    page_count = dec_table.shape[1]
    peer_count = lax.axis_size("col")
    slot_count = max(2, (dec_count + peer_count - 1) // peer_count)
    holder = dec_holder[:, 0]
    onehot = (holder[:, None] == jnp.arange(peer_count)[None, :]).astype(jnp.int32)
    slot_rank = jnp.sum((jnp.cumsum(onehot, axis=0) - onehot) * onehot, axis=1)
    target = holder * slot_count + slot_rank
    int_facts = jnp.concatenate([dec_table, dec_len[:, None], dec_variate[:, None]], axis=1)
    all_slots = peer_count * slot_count
    to_slot = target[None, :] == jnp.arange(all_slots)[:, None]
    send_int = jnp.sum(jnp.where(to_slot[:, :, None], int_facts[None], 0), axis=1)
    send_int = send_int.reshape(peer_count, slot_count, page_count + 2)
    int_part = lax.all_to_all(send_int, "col", split_axis=0, concat_axis=0, tiled=True)
    slot_ints = int_part.reshape(all_slots, page_count + 2)
    slot_table = slot_ints[:, :page_count]
    slot_len = slot_ints[:, page_count]
    slot_variate = slot_ints[:, page_count + 1]
    last_place = (slot_len // page_size)[:, None] == jnp.arange(page_count)[None, :]
    last_page = jnp.sum(jnp.where(last_place, slot_table, 0), axis=1)
    my_col = lax.axis_index("col")
    shift_peer = (my_col + jnp.arange(peer_count)) % peer_count
    shift_page = jnp.sum(
        jnp.where(
            (shift_peer[:, None] == jnp.arange(peer_count)[None, :])[:, :, None],
            last_page.reshape(1, peer_count, slot_count),
            0,
        ),
        axis=1,
    ).reshape(-1)

    places = jnp.concatenate([segment_time(pre_variate[0]), dec_len]).astype(jnp.float32)
    spacing = jnp.arange(HD // 2).astype(jnp.float32) * (2.0 / HD)
    angles = places[:, None] * jnp.power(10000.0, -spacing)[None, :]
    cosines = jnp.tile(jnp.cos(angles), (1, 2 * heads_here))
    sines = jnp.tile(jnp.sin(angles), (1, 2 * heads_here))

    used_rows = slot_count * heads_here
    slot_rows = -(-used_rows // 8) * 8

    def per_row(values):
        wide = jnp.broadcast_to(
            values.reshape(peer_count, slot_count, 1, -1),
            (peer_count, slot_count, heads_here, values.shape[-1]),
        ).reshape(peer_count, used_rows, -1)
        wide = jnp.pad(wide, ((0, 0), (0, slot_rows - used_rows), (0, 0)))
        return wide.reshape(peer_count * slot_rows, -1)

    facts = per_row(slot_ints)
    bias_pair = jnp.stack([bias_same, bias_diff], axis=1)
    slot_bias = jnp.tile(
        jnp.pad(jnp.tile(bias_pair, (slot_count, 1)), ((0, slot_rows - used_rows), (0, 0))),
        (peer_count, 1),
    )
    placed = per_row(to_slot.astype(jnp.float32))
    hidden, flat_key, flat_value, tail_back = whole_layer(
        (
            peer_count,
            lax.axis_size("row"),
            heads_here,
            dec_count,
            page_count,
            score_scale,
            slot_count,
        ),
        (
            jnp.stack([bias_same, bias_diff]),
            shift_page,
            pre_variate[0][:, None],
            pre_variate,
            pre_keep,
            facts,
            slot_bias,
            jnp.repeat(bias_same, HD)[None],
            page_variates,
            placed.T,
            placed.astype(jnp.bfloat16),
            cosines,
            sines,
            jnp.stack([q_gain, k_gain]),
            jnp.stack([norm1, norm2]),
            layer_input,
            kv_pool,
        ),
        (w_q, w_k, w_v, w_o, w_gate, w_up, w_down),
    )
    tail_at = ((my_col - holder) % peer_count) * slot_count + slot_rank
    old_tails = tail_back.reshape(all_slots, 2, page_size, local_width)[tail_at]
    hit_row = (jnp.arange(page_size)[None, :] == (dec_len % page_size)[:, None])[:, None, :, None]
    new_rows = jnp.stack([flat_key[pre_len:], flat_value[pre_len:]], axis=1)[:, :, None, :]
    tail_pages = jnp.where(hit_row, new_rows, old_tails)
    prefill_pages = jnp.stack(
        [
            flat_key[:pre_len].reshape(pre_len // page_size, page_size, local_width),
            flat_value[:pre_len].reshape(pre_len // page_size, page_size, local_width),
        ],
        axis=1,
    )
    return (hidden, prefill_pages, tail_pages)


def solution(mesh):
    placed = (
        P("col", "row"),
        P("col", "row"),
        P("col", "row"),
        P("col", "row"),
        P("row", "col"),
        P("col", "row"),
        P("col", "row"),
        P("row", "col"),
        P(),
        P(),
        P("row"),
        P("row"),
        P("row"),
        P("row"),
        P("col", None),
        P("col", None),
        P("col"),
        P("col"),
        P("col", None),
        P("col", None),
        P("col", None, None, "row"),
        P("col", None),
    )
    return jax.shard_map(
        on_device,
        mesh=mesh,
        in_specs=placed,
        out_specs=(P("col", "row"), P("col", None, None, "row"), P("col", None, None, "row")),
        check_vma=False,
    )
```
